512 devices in a mesh: gx: 8 (over x, core), gy: 8 (over z_hi, y), gz: 8 (over z_lo).
Axes of the slice: x: 4, y: 4, z: 16 (z_hi: 2, z_lo: 8; z = z_hi * 8 + z_lo), core: 2. Of those that a mesh axis runs over, the one named last changes fastest.
Arguments:
- charge: bfloat16 [128, 256, 1024], P('gx', 'gy', 'gz'), may hold values from -6 to 6
- kernel_taps: float32 [2, 17], replicated, may hold values from 0 to 1, as said below
- top_x: float32 [32], replicated, may hold values from 0 to 1, as said below
- top_y: float32 [64], replicated, may hold values from 0 to 1, as said below
- top_z: float32 [256], replicated, may hold values from 0 to 1, as said below
Outputs:
- potential: float32 [128, 256, 1024], P('gx', 'gy', 'gz')
The draws below stay inside these ranges and needn't reach their ends.
Inputs may be any that keep to these rules, and one draw needn't show every extreme that they name: `kernel_taps`: positive taps. `top_x`: positive. `top_y`: positive. `top_z`: positive.
All inputs are finite; a program needn't handle non-finite values.
Results may differ from the reference program's by a relative error of at most 0.00041.
Values may be sent and summed in bfloat16 or wider, within the bound.
No kernel may reach another device: no remote copies, remote signals or barrier semaphores. Data moves between devices by JAX's collectives and lax.ppermute only.
A program may use at most 64 MiB of HBM per device.

```python
import jax
import jax.numpy as jnp
from jax import lax

RADIUS = 8
LEVELS = 2
NX = 128
NY = 256
NZ = 1024


def periodic_profile(key, length_now, spread, scale, low_end, high_end):
    places = jnp.arange(length_now, dtype=jnp.float32)
    distance = jnp.minimum(places, length_now - places)
    rough = jax.random.uniform(key, (length_now,), jnp.float32, low_end, high_end)
    return scale * rough * jnp.exp(-distance * distance / (2.0 * spread * spread))


def top_profile(key, length_now, low_end, high_end):
    spread = length_now / 4.0
    scale = 0.5 / jnp.sqrt(spread * 1.7725)
    return periodic_profile(key, length_now, spread, scale, low_end, high_end)


def draw_kernel_taps(key, part):
    key = jax.random.fold_in(key, 1)
    low_end, high_end = (0.5, 1.5)
    offsets = jnp.arange(2 * RADIUS + 1, dtype=jnp.float32) - RADIUS
    spreads = 3.0 + jnp.arange(LEVELS, dtype=jnp.float32)[:, None]
    rough = jax.random.uniform(key, (LEVELS, 2 * RADIUS + 1), jnp.float32, low_end, high_end)
    return 0.45 * rough * jnp.exp(-offsets[None, :] ** 2 / (2.0 * spreads * spreads))


def draw_top_x(key, part):
    key = jax.random.fold_in(key, 2)
    return top_profile(key, NX // 4, 0.5, 1.5)


def draw_top_y(key, part):
    key = jax.random.fold_in(key, 3)
    return top_profile(key, NY // 4, 0.5, 1.5)


def draw_top_z(key, part):
    key = jax.random.fold_in(key, 4)
    return top_profile(key, NZ // 4, 0.5, 1.5)


def block_scale(rng, dims, cuts, smallest, largest):
    loudness, own = 1.0, jax.random.fold_in(rng, 6)
    for axis_at, shards_of in cuts:
        steps = jnp.exp(jax.random.uniform(jax.random.fold_in(own, axis_at), (shards_of,), jnp.float32, smallest / len(cuts), largest / len(cuts)))
        loudness = loudness * jnp.repeat(steps, dims[axis_at] // shards_of).reshape([-1 if axis == axis_at else 1 for axis in range(len(dims))])
    return loudness


def normal_values(stream_key, extent, width, limit, split=(), kind=jnp.bfloat16):
    array = width * jax.random.normal(stream_key, extent, jnp.float32)
    if split:
        array = array * block_scale(stream_key, extent, split, -0.22, 0.18)
    return jnp.clip(array, -limit, limit).astype(kind)


def setup_inputs(seed: int = 0) -> dict:
    arg_keys = jax.random.split(jax.random.key(seed), 6)
    return {
        "charge": normal_values(arg_keys[0], (NX, NY, NZ), 1.0, 6.0, ((0, 8), (1, 8), (2, 8))),
        "kernel_taps": draw_kernel_taps(jax.random.fold_in(arg_keys[5], 71), 0),
        "top_x": draw_top_x(jax.random.fold_in(arg_keys[5], 71), 0),
        "top_y": draw_top_y(jax.random.fold_in(arg_keys[5], 71), 0),
        "top_z": draw_top_z(jax.random.fold_in(arg_keys[5], 71), 0),
    }


spread_weights = (-1.0 / 16.0, 0.0, 9.0 / 16.0, 1.0, 9.0 / 16.0, 0.0, -1.0 / 16.0)


def convolve_axis(field, taps_row, axis):
    summed = jnp.zeros_like(field)
    for offset in range(-RADIUS, RADIUS + 1):
        summed = summed + taps_row[offset + RADIUS] * jnp.roll(field, -offset, axis)
    return summed


def restrict_axis(field, axis):
    summed = jnp.zeros_like(field)
    for offset in range(-3, 4):
        summed = summed + spread_weights[offset + 3] * jnp.roll(field, -offset, axis)
    return lax.slice_in_dim(summed, 0, field.shape[axis], 2, axis)


def prolong_axis(field, axis):
    zeros = jnp.zeros_like(field)
    stacked = jnp.stack([field, zeros], axis=axis + 1)
    new_shape = list(field.shape)
    new_shape[axis] = 2 * field.shape[axis]
    upsampled = stacked.reshape(new_shape)
    summed = jnp.zeros_like(upsampled)
    for offset in range(-3, 4):
        summed = summed + spread_weights[offset + 3] * jnp.roll(upsampled, offset, axis)
    return summed


def circulant(profile):
    length_now = profile.shape[0]
    places = jnp.arange(length_now, dtype=jnp.int32)
    index_table = (places[:, None] - places[None, :]) % length_now
    return profile[index_table]


def reference(charge, kernel_taps, top_x, top_y, top_z):
    highest = lax.Precision.HIGHEST
    field = charge.astype(jnp.float32)
    nears = []
    for section in range(LEVELS):
        near = field
        for axis in range(3):
            near = convolve_axis(near, kernel_taps[section], axis)
        nears.append(near)
        for axis in range(3):
            field = restrict_axis(field, axis)
    coarse = lax.optimization_barrier(field.astype(jnp.bfloat16)).astype(jnp.float32)
    result = jnp.einsum('xyz,cz->xyc', coarse, circulant(top_z), precision=highest)
    result = jnp.einsum('xyc,by->xbc', result, circulant(top_y), precision=highest)
    result = jnp.einsum('xbc,ax->abc', result, circulant(top_x), precision=highest)
    for section in range(LEVELS - 1, -1, -1):
        raised = result
        for axis in range(3):
            raised = prolong_axis(raised, axis)
        result = nears[section] + raised
    return result
```

```python
import jax
import jax.numpy as jnp
import numpy as np
from jax import lax
from jax.experimental import pallas as pl
from jax.experimental.pallas import tpu as pltpu
from jax.sharding import PartitionSpec as P

f32 = jnp.float32
bf16 = jnp.bfloat16
highest = lax.Precision.HIGHEST
weight = {-3: -1.0 / 16.0, -1: 9.0 / 16.0, 0: 1.0, 1: 9.0 / 16.0, 3: -1.0 / 16.0}

twice = {}
for d0, w0 in weight.items():
    for d1, w1 in weight.items():
        twice[d0 + 2 * d1] = twice.get(d0 + 2 * d1, 0.0) + w0 * w1

swap_even = [(0, 1), (1, 0), (2, 3), (3, 2), (4, 5), (5, 4), (6, 7), (7, 6)]
swap_odd = [(1, 2), (2, 1), (3, 4), (4, 3), (5, 6), (6, 5), (7, 0), (0, 7)]


def table(rows, cols, entry):
    return np.array([[entry(r, c) for c in range(cols)] for r in range(rows)], np.float32)


def z_cell(row, width):
    if row < 128:
        return row
    if row < 128 + width:
        return row - 128 - width
    if row < 128 + 2 * width:
        return row - width
    return None


def z_twice(row, col):
    cell = z_cell(row, 32)
    return 0.0 if cell is None else twice.get(cell - 4 * (col % 32), 0.0)


y_twice = table(8, 64, lambda r, c: twice.get(c - 16 - 4 * r, 0.0))
z_twice_matrix = table(256, 128, z_twice)
y_raise_top = table(24, 16, lambda r, c: weight.get((r - 1) - 2 * (c - 2), 0.0) if r < 19 and c < 13 else 0.0)
z_raise_top = table(128, 128, lambda r, c: weight.get((c - 1) - 2 * (r - 2), 0.0) if r < 37 and c < 67 else 0.0)
y_raise = table(32, 24, lambda r, c: weight.get(r - 2 * (c - 1), 0.0) if c < 19 else 0.0)
z_raise = table(128, 128, lambda r, c: weight.get(c - 2 * (r - 1), 0.0) if r < 67 else 0.0)


def dot(a, b):
    return jnp.dot(a, b, precision=highest, preferred_element_type=f32)


def lanes(parts):
    return jnp.concatenate(parts, axis=1)


def iota(shape, dim):
    return lax.broadcasted_iota(jnp.int32, shape, dim)


def call(body, outs, args, smem=(), scratch=(), flops=1_000_000, bytes_accessed=1_000_000):
    return pl.pallas_call(
        body,
        out_shape=[jax.ShapeDtypeStruct(s, d) for s, d in outs],
        in_specs=[
            pl.BlockSpec(memory_space=pltpu.SMEM if i in smem else pltpu.VMEM)
            for i in range(len(args))
        ],
        out_specs=[pl.BlockSpec(memory_space=pltpu.VMEM) for _ in outs],
        scratch_shapes=list(scratch),
        compiler_params=pltpu.CompilerParams(vmem_limit_bytes=32 * 1024 * 1024),
        cost_estimate=pl.CostEstimate(
            flops=flops, bytes_accessed=bytes_accessed, transcendentals=0
        ),
    )(*args)


def pair_taps(taps):
    merged = {}
    for b in range(-8, 9):
        for d, w in weight.items():
            merged.setdefault(2 * b + d, []).append(w * taps[1, b + 8])
    return {m: sum(terms[1:], terms[0]) for m, terms in merged.items()}


def prep_near(taps, my1, my2, mz1, mz2):
    merged = pair_taps(taps)

    def fill(gap, values):
        out = jnp.zeros(gap.shape, f32)
        for m, value in values.items():
            out = jnp.where(gap == m, value, out)
        return out

    single = {m: taps[0, m + 8] for m in range(-8, 9)}
    my1[...] = fill(iota((32, 48), 1) - 8 - iota((32, 48), 0), single)
    my2[...] = fill(iota((24, 80), 1) - 24 - 2 * (iota((24, 80), 0) - 1), merged)
    far_off = 1 << 20

    def z_cells(width):
        row = iota((256, 128), 0)
        cell = jnp.where(row < 128, row, jnp.where(row < 128 + width, row - 128 - width, row - width))
        return jnp.where(row < 128 + 2 * width, cell, far_off)

    mz1[...] = fill(z_cells(8) - iota((256, 128), 1), single)
    mz2[...] = fill(z_cells(32) - 2 * (iota((256, 128), 1) - 1), merged)


def toeplitz(profile, shift, size):
    start = pltpu.roll(jnp.broadcast_to(profile, (8, size)), shift, 1)[0:1]
    return pltpu.roll(jnp.broadcast_to(start, (size, size)), 0, 1, stride=1, stride_axis=0)


def prep_top(where, top_x, top_y, top_z, wz1, wz2, wz3, my, wx):
    gx, gy, gz = where[0], where[1], where[2]
    tz = toeplitz(top_z[...], lax.rem(258 - 32 * gz, 256), 256)
    lane = iota((256, 256), 1)
    near = jnp.where(lane < 64, tz, 0.0)
    blocks = [near] + [pltpu.roll(near, 64 * a, 1) for a in range(1, 4)]
    for g in range(8):
        for a in range(4):
            rows = pl.ds(128 * g + 32 * a, 32)
            part = blocks[a][32 * g : 32 * g + 32]
            first = part.astype(bf16)
            rest = part - first.astype(f32)
            second = rest.astype(bf16)
            wz1[rows, :] = first
            wz2[rows, :] = second
            wz3[rows, :] = (rest - second.astype(f32)).astype(bf16)
    ty = toeplitz(top_y[...], lax.rem(130 - 8 * gy, 128), 128)
    my[...] = ty.T[0:16, 0:64]
    tx = toeplitz(top_x[...], lax.rem(130 - 4 * gx, 128), 128)
    spread = jnp.where(iota((32, 2048), 1) // 64 == iota((32, 2048), 0), 1.0, 0.0)
    wx[...] = dot(tx.T[0:16, 0:32], spread)


def x_step(where, taps, lo2, lo1, own, hi1, hi2, n1, n2, q3, out_even, out_odd, ext):
    at = 0
    for part in (lo2, lo1, own, hi1, hi2):
        count = part.shape[0]
        ext[at : at + count] = part[...].astype(f32)
        at += count
    for t in range(4):
        rows = pl.ds(8 * t, 8)
        f = {r: ext[r + 22, rows, :] for r in range(-22, 38)}
        for i in range(16):
            total = taps[0, 0] * f[i - 8]
            for a in range(-7, 9):
                total = total + taps[0, a + 8] * f[i + a]
            n1[i, rows, :] = total
        half = {
            j: f[2 * j]
            + (9.0 / 16.0) * (f[2 * j - 1] + f[2 * j + 1])
            - (1.0 / 16.0) * (f[2 * j - 3] + f[2 * j + 3])
            for j in range(-9, 18)
        }
        for i in range(-1, 10):
            total = taps[1, 0] * half[i - 8]
            for a in range(-7, 9):
                total = total + taps[1, a + 8] * half[i + a]
            n2[i + 1, rows, :] = total
        for j in range(4):
            q3[j, rows, :] = (
                half[2 * j]
                + (9.0 / 16.0) * (half[2 * j - 1] + half[2 * j + 1])
                - (1.0 / 16.0) * (half[2 * j - 3] + half[2 * j + 3])
            )
    odd = lax.rem(where[1], 2)
    for out, low in ((out_even, odd), (out_odd, 1 - odd)):
        for i in range(16):
            out[8 * i : 8 * i + 8] = n1[i, pl.ds(pl.multiple_of(24 * (1 - low), 8), 8), :]
        for i in range(11):
            out[128 + 24 * i : 152 + 24 * i] = n2[i, pl.ds(pl.multiple_of(8 * (1 - low), 8), 24), :]
        for i in range(4):
            out[392 + 16 * i : 408 + 16 * i] = q3[i, pl.ds(pl.multiple_of(16 * (1 - low), 8), 16), :]


def pick(is_odd, even_ref, odd_ref, rows):
    even_part, odd_part = even_ref[rows, :], odd_ref[rows, :]
    low = jnp.where(is_odd, even_part, odd_part)
    high = jnp.where(is_odd, odd_part, even_part)
    return low, high


def y_step(where, n1, n2, q3, from_even, from_odd, my1, my2, my3, n1_out, n2_out, q3_out, out_even, out_odd):
    is_odd = lax.rem(where[1], 2) == 1

    def columns(ref, count, at, width):
        parts = []
        for i in range(count):
            low, high = pick(is_odd, from_even, from_odd, pl.ds(at + width * i, width))
            parts.append(jnp.concatenate([low, ref[i], high], axis=0))
        return lanes(parts)

    r1 = dot(my1[...], columns(n1, 16, 0, 8))
    r2 = dot(my2[...], columns(n2, 11, 128, 24))
    r3 = dot(my3[...], columns(q3, 4, 392, 16))
    parts1 = [r1[:, 128 * i : 128 * i + 128] for i in range(16)]
    parts2 = [r2[:, 128 * i : 128 * i + 128] for i in range(11)]
    parts3 = [r3[:, 128 * i : 128 * i + 128] for i in range(4)]
    for i in range(16):
        n1_out[i] = parts1[i]
    for i in range(11):
        n2_out[i] = parts2[i]
    for i in range(4):
        q3_out[i] = parts3[i]

    def pack(parts, width, high):
        lane = iota(parts[0].shape, 1) // width
        out = jnp.zeros(parts[0].shape, f32)
        for s, part in enumerate(parts):
            shift = (width * s + (width if high else 0)) % 128
            moved = part if shift == 0 else pltpu.roll(part, shift, 1)
            out = jnp.where(lane == s, moved, out)
        return out

    def packed(high):
        groups = [pack(parts1, 8, high)]
        groups += [pack(parts2[4 * g : 4 * g + 4], 32, high) for g in range(3)]
        groups += [pack(parts3, 32, high)]
        return jnp.concatenate(groups, axis=0)

    z_odd = lax.rem(where[2], 2) == 1
    low, high = packed(False), packed(True)
    out_even[...] = jnp.where(z_odd, low, high)
    out_odd[...] = jnp.where(z_odd, high, low)


def windows(low, high, slot, width):
    down = (128 - width * slot) % 128
    up = (128 + width - width * slot) % 128
    low = low if down == 0 else pltpu.roll(low, down, 1)
    high = high if up == 0 else pltpu.roll(high, up, 1)
    return jnp.where(iota(low.shape, 1) < width, low, high)


def q3_step(where, q3, from_even, from_odd, mz3, out):
    z_odd = lax.rem(where[2], 2) == 1
    low, high = pick(z_odd, from_even, from_odd, pl.ds(104, 8))
    rows = jnp.concatenate([lanes([q3[a], windows(low, high, a, 32)]) for a in range(4)], axis=0)
    full = dot(rows, mz3[...])
    lane = iota((8, 128), 1) // 32
    block = full[0:8]
    for a in range(1, 4):
        block = jnp.where(lane == a, full[8 * a : 8 * a + 8], block)
    out[...] = jnp.broadcast_to(block.astype(bf16)[None], (64, 8, 128))


def near_step(where, n1, n2, from_even, from_odd, mz1, mz2, n1_out, n2_out):
    z_odd = lax.rem(where[2], 2) == 1
    low, high = pick(z_odd, from_even, from_odd, pl.ds(0, 32))
    rows = jnp.concatenate([lanes([n1[i], windows(low, high, i, 8)]) for i in range(16)], axis=0)
    n1_out[...] = dot(rows, mz1[...]).reshape(16, 32, 128)
    rows = []
    for g in range(3):
        low, high = pick(z_odd, from_even, from_odd, pl.ds(32 + 24 * g, 24))
        for s in range(4):
            if 4 * g + s < 11:
                rows.append(lanes([n2[4 * g + s], windows(low, high, s, 32)]))
    n2_out[...] = dot(jnp.concatenate(rows, axis=0), mz2[...]).reshape(11, 24, 128)


def top_step(gathered, wz1, wz2, wz3, my, out):
    whole = gathered[...].astype(f32).reshape(8, 8, 8, 128)
    rows = lanes([whole[:, g].reshape(64, 128) for g in range(8)]).astype(bf16)
    along_z = jnp.dot(rows, wz1[...], preferred_element_type=f32)
    along_z = along_z + jnp.dot(rows, wz2[...], preferred_element_type=f32)
    along_z = along_z + jnp.dot(rows, wz3[...], preferred_element_type=f32)
    out[...] = jnp.broadcast_to(dot(my[...], along_z)[None], (8, 16, 256))


def raise_rows(rows, first, last):
    out = {}
    for i in range(first, last + 1):
        if i % 2 == 0:
            out[i] = rows[i // 2]
        else:
            j = (i - 1) // 2
            out[i] = (9.0 / 16.0) * (rows[j] + rows[j + 1]) - (1.0 / 16.0) * (rows[j - 1] + rows[j + 2])
    return out


def last_step(top, wx, n1, n2, y1, z1, y2, z2, out):
    e3 = {}
    for i in range(9):
        total = None
        for g in range(8):
            for h in range(2):
                at = 256 * g + 128 * h
                term = wx[i : i + 1, at : at + 128] * top[g, :, 128 * h : 128 * h + 128]
                total = term if total is None else total + term
        e3[i - 2] = total + pltpu.roll(total, 64, 1)
    e2 = raise_rows(e3, -1, 9)
    wide = dot(y1[...], lanes([e2[i] for i in range(-1, 10)]))
    tall = jnp.concatenate([wide[:, 128 * i : 128 * i + 128] for i in range(11)], axis=0)
    tall = dot(tall, z1[...]) + n2[...].reshape(264, 128)
    tall = dot(tall, z2[...])
    wide = dot(y2[...], lanes([tall[24 * i : 24 * i + 24] for i in range(11)]))
    rows = raise_rows({i - 1: wide[:, 128 * i : 128 * i + 128] for i in range(11)}, 0, 15)
    for i in range(16):
        out[i] = rows[i] + n1[i]


def per_device(charge, kernel_taps, top_x, top_y, top_z):
    where = jnp.stack([lax.axis_index("gx"), lax.axis_index("gy"), lax.axis_index("gz")]).astype(jnp.int32)

    def shift(block, by):
        return lax.ppermute(block, "gx", [(i, (i + by) % 8) for i in range(8)])

    lo1 = shift(charge, 1)
    hi1 = shift(charge, -1)
    lo2 = shift(charge[10:16], 2)
    hi2 = shift(charge[0:6], -2)

    my1, my2, mz1, mz2 = call(
        prep_near,
        [((32, 48), f32), ((24, 80), f32), ((256, 128), f32), ((256, 128), f32)],
        [kernel_taps], smem=(0,),
    )
    wz1, wz2, wz3, my, wx = call(
        prep_top,
        [((1024, 256), bf16)] * 3 + [((16, 64), f32), ((16, 2048), f32)],
        [where, jnp.tile(top_x, 4)[None], jnp.tile(top_y, 2)[None], top_z[None]], smem=(0,),
    )

    n1, n2, q3, to_even, to_odd = call(
        x_step,
        [((16, 32, 128), f32), ((11, 32, 128), f32), ((4, 32, 128), f32), ((456, 128), f32), ((456, 128), f32)],
        [where, kernel_taps, lo2, lo1, charge, hi1, hi2], smem=(0, 1),
        scratch=[pltpu.VMEM((60, 32, 128), f32)],
    )
    from_even = lax.ppermute(to_even, "gy", swap_even)
    from_odd = lax.ppermute(to_odd, "gy", swap_odd)

    n1, n2, q3, to_even, to_odd = call(
        y_step,
        [((16, 32, 128), f32), ((11, 24, 128), f32), ((4, 8, 128), f32), ((112, 128), f32), ((112, 128), f32)],
        [where, n1, n2, q3, from_even, from_odd, my1, my2, jnp.asarray(y_twice)], smem=(0,),
    )
    from_even = lax.ppermute(to_even, "gz", swap_even)
    from_odd = lax.ppermute(to_odd, "gz", swap_odd)

    (message,) = call(
        q3_step, [((64, 8, 128), bf16)],
        [where, q3, from_even, from_odd, jnp.asarray(z_twice_matrix)], smem=(0,),
    )
    gathered = lax.all_to_all(message, ("gy", "gz"), split_axis=0, concat_axis=0, tiled=True)
    n1, n2 = call(
        near_step, [((16, 32, 128), f32), ((11, 24, 128), f32)],
        [where, n1, n2, from_even, from_odd, mz1, mz2], smem=(0,),
    )
    (message,) = call(top_step, [((8, 16, 256), f32)], [gathered, wz1, wz2, wz3, my])
    top = lax.all_to_all(message, "gx", split_axis=0, concat_axis=0, tiled=True)
    (result,) = call(
        last_step, [((16, 32, 128), f32)],
        [top, wx, n1, n2, jnp.asarray(y_raise_top), jnp.asarray(z_raise_top), jnp.asarray(y_raise), jnp.asarray(z_raise)],
    )
    return result


def solution(mesh):
    return jax.shard_map(
        per_device,
        mesh=mesh,
        in_specs=(P("gx", "gy", "gz"), P(), P(), P(), P()),
        out_specs=P("gx", "gy", "gz"),
        check_vma=False,
    )
```

```python
import jax
import jax.numpy as jnp
import numpy as np
from jax import lax
from jax.experimental import pallas as pl
from jax.experimental.pallas import tpu as pltpu
from jax.sharding import PartitionSpec as P

f32 = jnp.float32
bf16 = jnp.bfloat16
highest = lax.Precision.HIGHEST
weight = {-3: -1.0 / 16.0, -1: 9.0 / 16.0, 0: 1.0, 1: 9.0 / 16.0, 3: -1.0 / 16.0}

twice = {}
for d0, w0 in weight.items():
    for d1, w1 in weight.items():
        twice[d0 + 2 * d1] = twice.get(d0 + 2 * d1, 0.0) + w0 * w1

swap_even = [(0, 1), (1, 0), (2, 3), (3, 2), (4, 5), (5, 4), (6, 7), (7, 6)]
swap_odd = [(1, 2), (2, 1), (3, 4), (4, 3), (5, 6), (6, 5), (7, 0), (0, 7)]


def table(rows, cols, entry):
    return np.array([[entry(r, c) for c in range(cols)] for r in range(rows)], np.float32)


def z_cell(row, width):
    if row < 128:
        return row
    if row < 128 + width:
        return row - 128 - width
    if row < 128 + 2 * width:
        return row - width
    return None


def z_twice16(row, col):
    cell = z_cell(row, 16)
    return 0.0 if cell is None else twice.get(cell - 4 * (col % 32), 0.0)


z_twice_matrix = table(256, 128, z_twice16)
y_raise_top = table(24, 16, lambda r, c: weight.get((r - 1) - 2 * (c - 2), 0.0) if r < 19 and c < 13 else 0.0)
z_raise_top = table(128, 128, lambda r, c: weight.get((c - 1) - 2 * (r - 2), 0.0) if r < 37 and c < 67 else 0.0)
y_raise = table(32, 24, lambda r, c: weight.get(r - 2 * (c - 1), 0.0) if c < 19 else 0.0)
z_raise = table(128, 128, lambda r, c: weight.get(c - 2 * (r - 1), 0.0) if r < 67 else 0.0)


def dot(a, b):
    return jnp.dot(a, b, precision=highest, preferred_element_type=f32)


def lanes(parts):
    return jnp.concatenate(parts, axis=1)


def iota(shape, dim):
    return lax.broadcasted_iota(jnp.int32, shape, dim)


def call(body, outs, args, smem=(), after=(), flops=1_000_000, bytes_accessed=1_000_000):
    def kernel(*refs):
        body(*refs[: len(args)], *refs[len(args) + len(after) :])

    return pl.pallas_call(
        kernel,
        out_shape=[jax.ShapeDtypeStruct(s, d) for s, d in outs],
        in_specs=[
            pl.BlockSpec(memory_space=pltpu.SMEM if i in smem else pltpu.VMEM)
            for i in range(len(args))
        ]
        + [pl.BlockSpec(memory_space=pl.ANY) for _ in after],
        out_specs=[pl.BlockSpec(memory_space=pltpu.VMEM) for _ in outs],
        compiler_params=pltpu.CompilerParams(vmem_limit_bytes=32 * 1024 * 1024),
        cost_estimate=pl.CostEstimate(
            flops=flops, bytes_accessed=bytes_accessed, transcendentals=0
        ),
        name=body.__name__,
    )(*args, *after)


def pair_taps(taps):
    merged = {}
    for b in range(-8, 9):
        for d, w in weight.items():
            merged.setdefault(2 * b + d, []).append(w * taps[1, b + 8])
    return {m: sum(terms[1:], terms[0]) for m, terms in merged.items()}


def fill(gap, values):
    out = jnp.zeros(gap.shape, f32)
    for m, value in values.items():
        out = jnp.where(gap == m, value, out)
    return out


def prep_y(taps, my):
    def gap(rows, first, step):
        return iota((rows, 80), 1) - 24 - step * (iota((rows, 80), 0) + first)

    single = {m: taps[0, m + 8] for m in range(-8, 9)}
    part = jnp.concatenate(
        [fill(gap(32, 0, 1), single), fill(gap(24, -1, 2), pair_taps(taps)), fill(gap(8, 0, 4), twice)], axis=0
    )
    first = part.astype(bf16)
    rest = part - first.astype(f32)
    second = rest.astype(bf16)
    third = (rest - second.astype(f32)).astype(bf16)
    my[...] = jnp.concatenate([first.astype(f32), second.astype(f32), third.astype(f32)], axis=0).astype(bf16)


def prep_z(taps, mz1, mz2):
    far_off = 1 << 20

    def z_cells(width):
        row = iota((256, 128), 0)
        cell = jnp.where(row < 128, row, jnp.where(row < 128 + width, row - 128 - width, row - width))
        return jnp.where(row < 128 + 2 * width, cell, far_off)

    single = {m: taps[0, m + 8] for m in range(-8, 9)}
    mz1[...] = fill(z_cells(8) - iota((256, 128), 1), single)
    mz2[...] = fill(z_cells(32) - 2 * (iota((256, 128), 1) - 1), pair_taps(taps))


def toeplitz(profile, shift, size):
    start = pltpu.roll(jnp.broadcast_to(profile, (8, size)), shift, 1)[0:1]
    return pltpu.roll(jnp.broadcast_to(start, (size, size)), 0, 1, stride=1, stride_axis=0)


def prep_top(top_x, top_y, top_z, wz1, wz2, wz3, my, wx):
    gx, gy, gz = lax.axis_index("gx"), lax.axis_index("gy"), lax.axis_index("gz")
    tz = toeplitz(top_z[...], lax.rem(258 - 32 * gz, 256), 256)
    lane = iota((256, 256), 1)
    near = jnp.where(lane < 64, tz, 0.0)
    blocks = [near] + [pltpu.roll(near, 64 * a, 1) for a in range(1, 4)]
    for g in range(8):
        for a in range(4):
            rows = pl.ds(128 * g + 32 * a, 32)
            part = blocks[a][32 * g : 32 * g + 32]
            first = part.astype(bf16)
            rest = part - first.astype(f32)
            second = rest.astype(bf16)
            wz1[rows, :] = first
            wz2[rows, :] = second
            wz3[rows, :] = (rest - second.astype(f32)).astype(bf16)
    ty = toeplitz(lanes([top_y[...]] * 2), lax.rem(130 - 8 * gy, 128), 128)
    my[...] = ty.T[0:16, 0:64]
    tx = toeplitz(lanes([top_x[...]] * 4), lax.rem(130 - 4 * gx, 128), 128)
    spread = jnp.where(iota((32, 2048), 1) // 64 == iota((32, 2048), 0), 1.0, 0.0)
    wx[...] = dot(tx.T[0:16, 0:32], spread)


def odd_place(axis):
    return lax.rem(lax.axis_index(axis), 2) == 1


def choose(is_odd, low, high):
    return jnp.where(is_odd, low, high), jnp.where(is_odd, high, low)


def y_send(own, out_even, out_odd):
    is_odd = odd_place("gy")
    cells = own[...].astype(f32)
    low = jnp.concatenate([cells[i, 0:24] for i in range(16)], axis=0)
    high = jnp.concatenate([cells[i, 8:32] for i in range(16)], axis=0)
    even, odd = choose(is_odd, low, high)
    out_even[...] = even.astype(bf16)
    out_odd[...] = odd.astype(bf16)


def y_step(own, from_even, from_odd, my, n1, n2, q3, out_even, out_odd):
    low, high = arrived("gy", from_even, from_odd, pl.ds(0, 384))
    low, high = low.astype(f32), high.astype(f32)
    cells = own[...].astype(f32)
    columns = lanes([
        jnp.concatenate([low[24 * i : 24 * i + 24], cells[i], high[24 * i : 24 * i + 24]], axis=0)
        for i in range(16)
    ])
    terms = jnp.dot(my[...], columns.astype(bf16), preferred_element_type=f32)
    done = terms[0:64] + (terms[64:128] + terms[128:192])
    parts = [done[:, 128 * i : 128 * i + 128] for i in range(16)]
    parts1 = [part[0:32] for part in parts]
    parts2 = [part[32:56] for part in parts]
    parts3 = [part[56:64] for part in parts]
    for i in range(16):
        n1[i] = parts1[i]
        n2[i] = parts2[i]
        q3[i] = parts3[i]

    def pack(parts, width, high):
        lane = iota(parts[0].shape, 1) // width
        out = jnp.zeros(parts[0].shape, f32)
        for s, part in enumerate(parts):
            shift = (width * s + (width if high else 0)) % 128
            moved = part if shift == 0 else pltpu.roll(part, shift, 1)
            out = jnp.where(lane == s, moved, out)
        return out

    def packed(high):
        groups = [pack(parts1, 8, high)]
        groups += [pack(parts2[4 * g : 4 * g + 4], 32, high) for g in range(4)]
        groups += [pack(parts3[8 * g : 8 * g + 8], 16, high) for g in range(2)]
        return jnp.concatenate(groups, axis=0)

    out_even[...], out_odd[...] = choose(odd_place("gz"), packed(False), packed(True))


def arrived(axis, from_even, from_odd, rows):
    is_odd = odd_place(axis)
    even_part, odd_part = from_even[rows, :], from_odd[rows, :]
    return jnp.where(is_odd, even_part, odd_part), jnp.where(is_odd, odd_part, even_part)


def windows(low, high, slot, width):
    down = (128 - width * slot) % 128
    up = (128 + width - width * slot) % 128
    low = low if down == 0 else pltpu.roll(low, down, 1)
    high = high if up == 0 else pltpu.roll(high, up, 1)
    return jnp.where(iota(low.shape, 1) < width, low, high)


def q3_z_step(q3, from_even, from_odd, mz3, out):
    rows = []
    for g in range(2):
        low, high = arrived("gz", from_even, from_odd, pl.ds(128 + 8 * g, 8))
        rows += [lanes([q3[8 * g + s], windows(low, high, s, 16)]) for s in range(8)]
    full = dot(jnp.concatenate(rows, axis=0), mz3[...])
    slot = iota((8, 128), 1) // 32
    for g in range(4):
        block = full[32 * g : 32 * g + 8]
        for s in range(1, 4):
            block = jnp.where(slot == s, full[32 * g + 8 * s : 32 * g + 8 * s + 8], block)
        out[8 * g : 8 * g + 8] = block


def q3_x_step(low, own, high, out):
    groups = {}
    for first, ref in ((-4, low), (0, own), (4, high)):
        for g in range(4):
            groups[first + g] = ref[8 * g : 8 * g + 8]
    slot = iota((8, 128), 1) // 32
    block = jnp.zeros((8, 128), f32)
    for j in range(4):
        total = jnp.zeros((8, 128), f32)
        for q in range(-3, 3):
            factor = fill(slot, {s: twice.get(4 * q + s, 0.0) for s in range(4)})
            total = total + factor * groups[j + q]
        total = total + pltpu.roll(total, 64, 1)
        total = total + pltpu.roll(total, 32, 1)
        block = jnp.where(slot == j, total, block)
    out[...] = jnp.broadcast_to(block.astype(bf16)[None], (64, 8, 128))


def near_z_step(n1, n2, from_even, from_odd, mz1, mz2, n1_out, n2_out, to_low, to_high, to_low2, to_high2):
    low, high = arrived("gz", from_even, from_odd, pl.ds(0, 32))
    rows = jnp.concatenate([lanes([n1[i], windows(low, high, i, 8)]) for i in range(16)], axis=0)
    done1 = dot(rows, mz1[...])
    n1_out[...] = done1.reshape(16, 32, 128)
    rows = []
    for g in range(4):
        low, high = arrived("gz", from_even, from_odd, pl.ds(32 + 24 * g, 24))
        rows += [lanes([n2[4 * g + s], windows(low, high, s, 32)]) for s in range(4)]
    done2 = dot(jnp.concatenate(rows, axis=0), mz2[...])
    n2_out[...] = done2.reshape(16, 24, 128)
    to_low[0:256] = done1[0:256]
    to_low[256:640] = done2
    to_high[0:256] = done1[256:512]
    to_high[256:640] = done2
    to_low2[...] = done2[0:144]
    to_high2[...] = done2[240:384]


def near_x_step(taps, n1, n2, low, high, low2, high2, n1_out, n2_out):
    for t in range(4):
        f = {}
        for i in range(8):
            f[i - 8] = low[32 * i + 8 * t : 32 * i + 8 * t + 8]
            f[i + 16] = high[32 * i + 8 * t : 32 * i + 8 * t + 8]
        for i in range(16):
            f[i] = n1[i, 8 * t : 8 * t + 8]
        for i in range(16):
            total = taps[0, 0] * f[i - 8]
            for a in range(-7, 9):
                total = total + taps[0, a + 8] * f[i + a]
            n1_out[i, 8 * t : 8 * t + 8] = total
    for t in range(3):
        f = {}
        for i in range(16):
            at = 256 + 24 * i + 8 * t
            f[i - 16] = low[at : at + 8]
            f[i + 16] = high[at : at + 8]
            f[i] = n2[i, 8 * t : 8 * t + 8]
        for i in range(6):
            at = 24 * i + 8 * t
            f[i - 22] = low2[at : at + 8]
            f[i + 32] = high2[at : at + 8]
        half = {
            j: f[2 * j]
            + (9.0 / 16.0) * (f[2 * j - 1] + f[2 * j + 1])
            - (1.0 / 16.0) * (f[2 * j - 3] + f[2 * j + 3])
            for j in range(-9, 18)
        }
        for i in range(-1, 10):
            total = taps[1, 0] * half[i - 8]
            for a in range(-7, 9):
                total = total + taps[1, a + 8] * half[i + a]
            n2_out[i + 1, 8 * t : 8 * t + 8] = total


def top_step(gathered, wz1, wz2, wz3, my, out):
    whole = gathered[...].astype(f32).reshape(8, 8, 8, 128)
    rows = lanes([whole[:, g].reshape(64, 128) for g in range(8)]).astype(bf16)
    along_z = jnp.dot(rows, wz1[...], preferred_element_type=f32)
    along_z = along_z + jnp.dot(rows, wz2[...], preferred_element_type=f32)
    along_z = along_z + jnp.dot(rows, wz3[...], preferred_element_type=f32)
    out[...] = jnp.broadcast_to(dot(my[...], along_z)[None], (8, 16, 256))


def raise_rows(rows, first, last):
    out = {}
    for i in range(first, last + 1):
        if i % 2 == 0:
            out[i] = rows[i // 2]
        else:
            j = (i - 1) // 2
            out[i] = (9.0 / 16.0) * (rows[j] + rows[j + 1]) - (1.0 / 16.0) * (rows[j - 1] + rows[j + 2])
    return out


def last_step(top, wx, n1, n2, y1, z1, y2, z2, out):
    e3 = {}
    for i in range(9):
        total = None
        for g in range(8):
            for h in range(2):
                at = 256 * g + 128 * h
                term = wx[i : i + 1, at : at + 128] * top[g, :, 128 * h : 128 * h + 128]
                total = term if total is None else total + term
        e3[i - 2] = total + pltpu.roll(total, 64, 1)
    e2 = raise_rows(e3, -1, 9)
    wide = dot(y1[...], lanes([e2[i] for i in range(-1, 10)]))
    tall = jnp.concatenate([wide[:, 128 * i : 128 * i + 128] for i in range(11)], axis=0)
    tall = dot(tall, z1[...]) + n2[...].reshape(264, 128)
    tall = dot(tall, z2[...])
    wide = dot(y2[...], lanes([tall[24 * i : 24 * i + 24] for i in range(11)]))
    rows = raise_rows({i - 1: wide[:, 128 * i : 128 * i + 128] for i in range(11)}, 0, 15)
    for i in range(16):
        out[i] = rows[i] + n1[i]


def per_device(charge, kernel_taps, top_x, top_y, top_z):
    def shift(block, by):
        return lax.ppermute(block, "gx", [(i, (i + by) % 8) for i in range(8)])

    to_even, to_odd = call(y_send, [((384, 128), bf16)] * 2, [charge])
    from_odd = lax.ppermute(to_odd, "gy", swap_odd)
    from_even = lax.ppermute(to_even, "gy", swap_even)
    (my,) = call(prep_y, [((192, 80), bf16)], [kernel_taps], smem=(0,))
    mz1, mz2 = call(prep_z, [((256, 128), f32)] * 2, [kernel_taps], smem=(0,))
    wz1, wz2, wz3, ty, wx = call(
        prep_top,
        [((1024, 256), bf16)] * 3 + [((16, 64), f32), ((16, 2048), f32)],
        [top_x[None], top_y[None], top_z[None]],
    )

    n1, n2, q3, to_even, to_odd = call(
        y_step,
        [((16, 32, 128), f32), ((16, 24, 128), f32), ((16, 8, 128), f32), ((144, 128), f32), ((144, 128), f32)],
        [charge, from_even, from_odd, my], after=[mz1, wx],
    )
    from_odd = lax.ppermute(to_odd, "gz", swap_odd)
    from_even = lax.ppermute(to_even, "gz", swap_even)

    (q3,) = call(
        q3_z_step, [((32, 128), f32)],
        [q3, from_even, from_odd, jnp.asarray(z_twice_matrix)],
    )
    (message,) = call(q3_x_step, [((64, 8, 128), bf16)], [shift(q3, 1), q3, shift(q3, -1)])
    gathered = lax.all_to_all(message, ("gy", "gz"), split_axis=0, concat_axis=0, tiled=True)

    n1, n2, to_low, to_high, to_low2, to_high2 = call(
        near_z_step,
        [((16, 32, 128), f32), ((16, 24, 128), f32)] + [((640, 128), f32)] * 2 + [((144, 128), f32)] * 2,
        [n1, n2, from_even, from_odd, mz1, mz2], after=[message],
    )
    n1, n2 = call(
        near_x_step, [((16, 32, 128), f32), ((11, 24, 128), f32)],
        [kernel_taps, n1, n2, shift(to_high, 1), shift(to_low, -1), shift(to_high2, 2), shift(to_low2, -2)],
        smem=(0,),
    )
    (message,) = call(top_step, [((8, 16, 256), f32)], [gathered, wz1, wz2, wz3, ty], after=[n1])
    top = lax.all_to_all(message, "gx", split_axis=0, concat_axis=0, tiled=True)
    (result,) = call(
        last_step, [((16, 32, 128), f32)],
        [top, wx, n1, n2, jnp.asarray(y_raise_top), jnp.asarray(z_raise_top), jnp.asarray(y_raise), jnp.asarray(z_raise)],
    )
    return result


def solution(mesh):
    return jax.shard_map(
        per_device,
        mesh=mesh,
        in_specs=(P("gx", "gy", "gz"), P(), P(), P(), P()),
        out_specs=P("gx", "gy", "gz"),
        check_vma=False,
    )
```

```python
import jax
import jax.numpy as jnp
import numpy as np
from jax import lax
from jax.experimental import pallas as pl
from jax.experimental.pallas import tpu as pltpu
from jax.sharding import PartitionSpec as P

f32 = jnp.float32
bf16 = jnp.bfloat16
highest = lax.Precision.HIGHEST
weight = {-3: -1.0 / 16.0, -1: 9.0 / 16.0, 0: 1.0, 1: 9.0 / 16.0, 3: -1.0 / 16.0}

twice = {}
for d0, w0 in weight.items():
    for d1, w1 in weight.items():
        twice[d0 + 2 * d1] = twice.get(d0 + 2 * d1, 0.0) + w0 * w1

swap_even = [(0, 1), (1, 0), (2, 3), (3, 2), (4, 5), (5, 4), (6, 7), (7, 6)]
swap_odd = [(1, 2), (2, 1), (3, 4), (4, 3), (5, 6), (6, 5), (7, 0), (0, 7)]


def table(rows, cols, entry):
    return np.array([[entry(r, c) for c in range(cols)] for r in range(rows)], np.float32)


def z_cell(row, width):
    if row < 128:
        return row
    if row < 128 + width:
        return row - 128 - width
    if row < 128 + 2 * width:
        return row - width
    return None


def z_twice16(row, col):
    cell = z_cell(row, 16)
    return 0.0 if cell is None else twice.get(cell - 4 * (col % 32), 0.0)


z_twice_matrix = table(256, 128, z_twice16)
y_raise_top = table(24, 16, lambda r, c: weight.get((r - 1) - 2 * (c - 2), 0.0) if r < 19 and c < 13 else 0.0)
z_raise_top = table(128, 128, lambda r, c: weight.get((c - 1) - 2 * (r - 2), 0.0) if r < 37 and c < 67 else 0.0)
y_raise = table(32, 24, lambda r, c: weight.get(r - 2 * (c - 1), 0.0) if c < 19 else 0.0)
z_raise = table(128, 128, lambda r, c: weight.get(c - 2 * (r - 1), 0.0) if r < 67 else 0.0)


def dot(a, b):
    return jnp.dot(a, b, precision=highest, preferred_element_type=f32)


def halves(x):
    first = x.astype(bf16)
    return first, (x - first.astype(f32)).astype(bf16)


def from_left(m, x):
    return sum(jnp.dot(m[...], term, preferred_element_type=f32) for term in halves(x))


def from_right(x, m):
    return sum(jnp.dot(term, m[...], preferred_element_type=f32) for term in halves(x))


def lanes(parts):
    return jnp.concatenate(parts, axis=1)


def iota(shape, dim):
    return lax.broadcasted_iota(jnp.int32, shape, dim)


def call(body, outs, args, smem=(), after=(), flops=1_000_000, bytes_accessed=1_000_000):

    def kernel(*refs):
        body(*refs[: len(args)], *refs[len(args) + len(after) :])

    return pl.pallas_call(
        kernel,
        out_shape=[jax.ShapeDtypeStruct(s, d) for s, d in outs],
        in_specs=[
            pl.BlockSpec(memory_space=pltpu.SMEM if i in smem else pltpu.VMEM)
            for i in range(len(args))
        ]
        + [pl.BlockSpec(memory_space=pl.ANY) for _ in after],
        out_specs=[pl.BlockSpec(memory_space=pltpu.VMEM) for _ in outs],
        compiler_params=pltpu.CompilerParams(vmem_limit_bytes=32 * 1024 * 1024),
        cost_estimate=pl.CostEstimate(
            flops=flops, bytes_accessed=bytes_accessed, transcendentals=0
        ),
        name=body.__name__,
    )(*args, *after)


def pair_taps(taps):
    merged = {}
    for b in range(-8, 9):
        for d, w in weight.items():
            merged.setdefault(2 * b + d, []).append(w * taps[1, b + 8])
    return {m: sum(terms[1:], terms[0]) for m, terms in merged.items()}


def fill(gap, values):
    out = jnp.zeros(gap.shape, f32)
    for m, value in values.items():
        out = jnp.where(gap == m, value, out)
    return out


def prep_y(taps, my):
    def gap(rows, first, step):
        column = iota((rows, 76), 1)
        cell = jnp.where(column < 32, column, jnp.where(column < 54, column - 54, column - 22))
        return cell - step * (iota((rows, 76), 0) + first)

    single = {m: taps[0, m + 8] for m in range(-8, 9)}
    part = jnp.concatenate(
        [fill(gap(32, 0, 1), single), fill(gap(24, -1, 2), pair_taps(taps)), fill(gap(8, 0, 4), twice)], axis=0
    )
    first = part.astype(bf16)
    rest = part - first.astype(f32)
    second = rest.astype(bf16)
    third = (rest - second.astype(f32)).astype(bf16)
    my[...] = jnp.concatenate([first.astype(f32), second.astype(f32), third.astype(f32)], axis=0).astype(bf16)


def prep_z(taps, mz1, mz2):
    far_off = 1 << 20

    def z_cells(width):
        row = iota((256, 128), 0)
        cell = jnp.where(row < 128, row, jnp.where(row < 128 + width, row - 128 - width, row - width))
        return jnp.where(row < 128 + 2 * width, cell, far_off)

    single = {m: taps[0, m + 8] for m in range(-8, 9)}
    mz1[...] = fill(z_cells(8) - iota((256, 128), 1), single)
    mz2[...] = fill(z_cells(32) - 2 * (iota((256, 128), 1) - 1), pair_taps(taps))


def toeplitz(profile, shift, size):
    start = pltpu.roll(jnp.broadcast_to(profile, (8, size)), shift, 1)[0:1]
    return pltpu.roll(jnp.broadcast_to(start, (size, size)), 0, 1, stride=1, stride_axis=0)


def prep_top(top_x, top_y, top_z, wz1, wz2, my, wx):
    gx, gy, gz = lax.axis_index("gx"), lax.axis_index("gy"), lax.axis_index("gz")
    tz = toeplitz(top_z[...], lax.rem(258 - 32 * gz, 256), 256)
    lane = iota((256, 256), 1)
    near = jnp.where(lane < 64, tz, 0.0)
    blocks = [near] + [pltpu.roll(near, 64 * a, 1) for a in range(1, 4)]
    for g in range(8):
        for a in range(4):
            rows = pl.ds(128 * g + 32 * a, 32)
            part = blocks[a][32 * g : 32 * g + 32]
            wz1[rows, :], wz2[rows, :] = halves(part)
    ty = toeplitz(lanes([top_y[...]] * 2), lax.rem(130 - 8 * gy, 128), 128)
    my[...] = ty.T[0:16, 0:64]
    tx = toeplitz(lanes([top_x[...]] * 4), lax.rem(130 - 4 * gx, 128), 128)
    spread = jnp.where(iota((32, 2048), 1) // 64 == iota((32, 2048), 0), 1.0, 0.0)
    wx[...] = dot(tx.T[0:16, 0:32], spread)


def odd_place(axis):
    return lax.rem(lax.axis_index(axis), 2) == 1


def choose(is_odd, low, high):
    return jnp.where(is_odd, low, high), jnp.where(is_odd, high, low)


def y_send(own, out_even, out_odd):
    is_odd = odd_place("gy")
    cells = own[...].astype(f32)
    low = jnp.concatenate([cells[i, 0:22] for i in range(16)], axis=0)
    high = jnp.concatenate([cells[i, 10:32] for i in range(16)], axis=0)
    even, odd = choose(is_odd, low, high)
    out_even[...] = even.astype(bf16)
    out_odd[...] = odd.astype(bf16)


def y_step(own, from_odd, from_even, my, n1, n2, q3, out_even, out_odd):
    low, high = arrived("gy", from_even, from_odd, pl.ds(0, 352))
    low, high = low.astype(f32), high.astype(f32)
    cells = own[...].astype(f32)
    columns = lanes([
        jnp.concatenate([cells[i], low[22 * i : 22 * i + 22], high[22 * i : 22 * i + 22]], axis=0)
        for i in range(16)
    ])
    terms = jnp.dot(my[...], columns.astype(bf16), preferred_element_type=f32)
    done = terms[0:64] + (terms[64:128] + terms[128:192])
    parts = [done[:, 128 * i : 128 * i + 128] for i in range(16)]
    parts1 = [part[0:32] for part in parts]
    parts2 = [part[32:56] for part in parts]
    parts3 = [part[56:64] for part in parts]
    for i in range(16):
        n1[i] = parts1[i]
        n2[i] = parts2[i]
        q3[i] = parts3[i]

    def pack(parts, width, high):
        lane = iota(parts[0].shape, 1) // width
        out = jnp.zeros(parts[0].shape, f32)
        for s, part in enumerate(parts):
            shift = (width * s + (width if high else 0)) % 128
            moved = part if shift == 0 else pltpu.roll(part, shift, 1)
            out = jnp.where(lane == s, moved, out)
        return out

    def packed(high):
        groups = [pack(parts1, 8, high)]
        groups += [pack(parts2[4 * g : 4 * g + 4], 32, high) for g in range(4)]
        groups += [pack(parts3[8 * g : 8 * g + 8], 16, high) for g in range(2)]
        return jnp.concatenate(groups, axis=0)

    out_even[...], out_odd[...] = choose(odd_place("gz"), packed(False), packed(True))


def arrived(axis, from_even, from_odd, rows):
    is_odd = odd_place(axis)
    even_part, odd_part = from_even[rows, :], from_odd[rows, :]
    return jnp.where(is_odd, even_part, odd_part), jnp.where(is_odd, odd_part, even_part)


def windows(low, high, slot, width):
    down = (128 - width * slot) % 128
    up = (128 + width - width * slot) % 128
    low = low if down == 0 else pltpu.roll(low, down, 1)
    high = high if up == 0 else pltpu.roll(high, up, 1)
    return jnp.where(iota(low.shape, 1) < width, low, high)


def q3_z_step(q3, from_odd, from_even, mz3, out):
    rows = []
    for g in range(2):
        low, high = arrived("gz", from_even, from_odd, pl.ds(128 + 8 * g, 8))
        rows += [lanes([q3[8 * g + s], windows(low, high, s, 16)]) for s in range(8)]
    full = dot(jnp.concatenate(rows, axis=0), mz3[...])
    slot = iota((8, 128), 1) // 32
    for g in range(4):
        block = full[32 * g : 32 * g + 8]
        for s in range(1, 4):
            block = jnp.where(slot == s, full[32 * g + 8 * s : 32 * g + 8 * s + 8], block)
        out[8 * g : 8 * g + 8] = block


def q3_x_step(low, own, high, out):
    groups = {}
    for first, ref in ((-4, low), (0, own), (4, high)):
        for g in range(4):
            groups[first + g] = ref[8 * g : 8 * g + 8]
    slot = iota((8, 128), 1) // 32
    block = jnp.zeros((8, 128), f32)
    for j in range(4):
        total = jnp.zeros((8, 128), f32)
        for q in range(-3, 3):
            factor = fill(slot, {s: twice.get(4 * q + s, 0.0) for s in range(4)})
            total = total + factor * groups[j + q]
        total = total + pltpu.roll(total, 64, 1)
        total = total + pltpu.roll(total, 32, 1)
        block = jnp.where(slot == j, total, block)
    pair = jnp.concatenate([block, block], axis=0).astype(bf16)
    out[...] = jnp.broadcast_to(pair[None], (32, 16, 128))


def near_z_step(n1, n2, from_odd, from_even, mz1, mz2, n1_out, n2_out, to_low, to_high, to_low2, to_high2):
    low, high = arrived("gz", from_even, from_odd, pl.ds(0, 32))
    rows = jnp.concatenate([lanes([n1[i], windows(low, high, i, 8)]) for i in range(16)], axis=0)
    done1 = dot(rows, mz1[...])
    n1_out[...] = done1.reshape(16, 32, 128)
    rows = []
    for g in range(4):
        low, high = arrived("gz", from_even, from_odd, pl.ds(32 + 24 * g, 24))
        rows += [lanes([n2[4 * g + s], windows(low, high, s, 32)]) for s in range(4)]
    done2 = dot(jnp.concatenate(rows, axis=0), mz2[...])
    to_low[0:256] = done1[0:256]
    to_high[0:256] = done1[256:512]
    for j in range(-1, 10):
        share = jnp.zeros((24, 128), f32)
        for d, w in weight.items():
            if 0 <= 2 * j + d < 16:
                share = share + w * done2[24 * (2 * j + d) : 24 * (2 * j + d) + 24]
        at = 256 + 24 * (j + 1)
        n2_out[j + 1] = share
        to_low[at : at + 24] = share
        to_high[at : at + 24] = share
        if j < 2:
            to_low2[24 * (j + 1) : 24 * (j + 1) + 24] = share
        if j > 6:
            to_high2[24 * (j - 7) : 24 * (j - 7) + 24] = share


def near_x_step(taps, n1, n2, low, high, low2, high2, n1_out, n2_out):
    for t in range(4):
        f = {}
        for i in range(8):
            f[i - 8] = low[32 * i + 8 * t : 32 * i + 8 * t + 8]
            f[i + 16] = high[32 * i + 8 * t : 32 * i + 8 * t + 8]
        for i in range(16):
            f[i] = n1[i, 8 * t : 8 * t + 8]
        for i in range(16):
            total = taps[0, 0] * f[i - 8]
            for a in range(-7, 9):
                total = total + taps[0, a + 8] * f[i + a]
            n1_out[i, 8 * t : 8 * t + 8] = total
    for t in range(3):
        half = {}
        for j in range(-1, 10):
            at = 256 + 24 * (j + 1) + 8 * t
            for place, part in ((j - 8, low[at : at + 8]), (j, n2[j + 1, 8 * t : 8 * t + 8]), (j + 8, high[at : at + 8])):
                half[place] = half[place] + part if place in half else part
        for k in range(3):
            at = 24 * k + 8 * t
            half[k - 9] = half[k - 9] + low2[at : at + 8]
            half[k + 15] = half[k + 15] + high2[at : at + 8]
        for i in range(-1, 10):
            total = taps[1, 0] * half[i - 8]
            for a in range(-7, 9):
                total = total + taps[1, a + 8] * half[i + a]
            n2_out[i + 1, 8 * t : 8 * t + 8] = total


def top_step(gathered, wz1, wz2, my, out):
    whole = gathered[...].astype(f32).reshape(8, 8, 8, 128)
    rows = lanes([whole[:, g].reshape(64, 128) for g in range(8)]).astype(bf16)
    along_z = jnp.dot(rows, wz1[...], preferred_element_type=f32)
    along_z = along_z + jnp.dot(rows, wz2[...], preferred_element_type=f32)
    out[...] = jnp.broadcast_to(dot(my[...], along_z)[None], (8, 16, 256))


def raise_rows(rows, first, last):
    out = {}
    for i in range(first, last + 1):
        if i % 2 == 0:
            out[i] = rows[i // 2]
        else:
            j = (i - 1) // 2
            out[i] = (9.0 / 16.0) * (rows[j] + rows[j + 1]) - (1.0 / 16.0) * (rows[j - 1] + rows[j + 2])
    return out


def last_step(top, wx, n1, n2, y1, z1, y2, z2, out):
    e3 = {}
    for i in range(9):
        total = None
        for g in range(8):
            for h in range(2):
                at = 256 * g + 128 * h
                term = wx[i : i + 1, at : at + 128] * top[g, :, 128 * h : 128 * h + 128]
                total = term if total is None else total + term
        e3[i - 2] = total + pltpu.roll(total, 64, 1)
    e2 = raise_rows(e3, -1, 9)
    wide = from_left(y1, lanes([e2[i] for i in range(-1, 10)]))
    tall = jnp.concatenate([wide[:, 128 * i : 128 * i + 128] for i in range(11)], axis=0)
    tall = from_right(tall, z1) + n2[...].reshape(264, 128)
    tall = from_right(tall, z2)
    wide = from_left(y2, lanes([tall[24 * i : 24 * i + 24] for i in range(11)]))
    rows = raise_rows({i - 1: wide[:, 128 * i : 128 * i + 128] for i in range(11)}, 0, 15)
    for i in range(16):
        out[i] = rows[i] + n1[i]


def per_device(charge, kernel_taps, top_x, top_y, top_z):
    def shift(block, by):
        return lax.ppermute(block, "gx", [(i, (i + by) % 8) for i in range(8)])

    to_even, to_odd = call(y_send, [((352, 128), bf16)] * 2, [charge])
    from_odd = lax.ppermute(to_odd, "gy", swap_odd)
    from_even = lax.ppermute(to_even, "gy", swap_even)
    (my,) = call(prep_y, [((192, 76), bf16)], [kernel_taps], smem=(0,))
    mz1, mz2 = call(prep_z, [((256, 128), f32)] * 2, [kernel_taps], smem=(0,))
    wz1, wz2, ty, wx = call(
        prep_top,
        [((1024, 256), bf16)] * 2 + [((16, 64), f32), ((16, 2048), f32)],
        [top_x[None], top_y[None], top_z[None]],
    )

    n1, n2, q3, to_even, to_odd = call(
        y_step,
        [((16, 32, 128), f32), ((16, 24, 128), f32), ((16, 8, 128), f32), ((144, 128), f32), ((144, 128), f32)],
        [charge, from_odd, from_even, my], after=[mz1, wx],
    )
    from_odd = lax.ppermute(to_odd, "gz", swap_odd)
    from_even = lax.ppermute(to_even, "gz", swap_even)

    (q3,) = call(
        q3_z_step, [((32, 128), f32)],
        [q3, from_odd, from_even, jnp.asarray(z_twice_matrix)],
    )
    (message,) = call(q3_x_step, [((32, 16, 128), bf16)], [shift(q3, 1), q3, shift(q3, -1)])
    gathered = lax.all_to_all(
        message.reshape(64, 8, 128), ("gy", "gz"), split_axis=0, concat_axis=0, tiled=True
    )
    n1, n2, to_low, to_high, to_low2, to_high2 = call(
        near_z_step,
        [((16, 32, 128), f32), ((11, 24, 128), f32)] + [((520, 128), f32)] * 2 + [((72, 128), f32)] * 2,
        [n1, n2, from_odd, from_even, mz1, mz2], after=[message],
    )
    halos = [shift(to_high, 1), shift(to_low, -1), shift(to_high2, 2), shift(to_low2, -2)]
    (message,) = call(top_step, [((8, 16, 256), f32)], [gathered, wz1, wz2, ty], after=halos)
    n1, n2 = call(
        near_x_step, [((16, 32, 128), f32), ((11, 24, 128), f32)],
        [kernel_taps, n1, n2, *halos], smem=(0,), after=[message],
    )
    top = lax.all_to_all(message, "gx", split_axis=0, concat_axis=0, tiled=True)
    (result,) = call(
        last_step, [((16, 32, 128), f32)],
        [top, wx, n1, n2, *(jnp.asarray(m, bf16) for m in (y_raise_top, z_raise_top, y_raise, z_raise))],
    )
    return result


def solution(mesh):
    return jax.shard_map(
        per_device,
        mesh=mesh,
        in_specs=(P("gx", "gy", "gz"), P(), P(), P(), P()),
        out_specs=P("gx", "gy", "gz"),
        check_vma=False,
    )
```

```python
import jax
import jax.numpy as jnp
import numpy as np
from jax import lax
from jax.experimental import pallas as pl
from jax.experimental.pallas import tpu as pltpu
from jax.sharding import PartitionSpec as P

f32 = jnp.float32
bf16 = jnp.bfloat16
highest = lax.Precision.HIGHEST
weight = {-3: -1.0 / 16.0, -1: 9.0 / 16.0, 0: 1.0, 1: 9.0 / 16.0, 3: -1.0 / 16.0}

twice = {}
for d0, w0 in weight.items():
    for d1, w1 in weight.items():
        twice[d0 + 2 * d1] = twice.get(d0 + 2 * d1, 0.0) + w0 * w1

swap_even = [(0, 1), (1, 0), (2, 3), (3, 2), (4, 5), (5, 4), (6, 7), (7, 6)]
swap_odd = [(1, 2), (2, 1), (3, 4), (4, 3), (5, 6), (6, 5), (7, 0), (0, 7)]


def table(rows, cols, entry):
    return np.array([[entry(r, c) for c in range(cols)] for r in range(rows)], np.float32)


def z_cell(row, width):
    if row < 128:
        return row
    if row < 128 + width:
        return row - 128 - width
    if row < 128 + 2 * width:
        return row - width
    return None


def z_twice16(row, col):
    cell = z_cell(row, 16)
    return 0.0 if cell is None else twice.get(cell - 4 * (col % 32), 0.0)


z_twice_matrix = table(256, 128, z_twice16)
y_raise_top = table(24, 16, lambda r, c: weight.get((r - 1) - 2 * (c - 2), 0.0) if r < 19 and c < 13 else 0.0)
z_raise_top = table(128, 128, lambda r, c: weight.get((c - 1) - 2 * (r - 2), 0.0) if r < 37 and c < 67 else 0.0)
y_raise = table(32, 24, lambda r, c: weight.get(r - 2 * (c - 1), 0.0) if c < 19 else 0.0)
z_raise = table(128, 128, lambda r, c: weight.get(c - 2 * (r - 1), 0.0) if r < 67 else 0.0)


def dot(a, b):
    return jnp.dot(a, b, precision=highest, preferred_element_type=f32)


def halves(x):
    first = x.astype(bf16)
    return first, (x - first.astype(f32)).astype(bf16)


def from_left(m, x):
    return sum(jnp.dot(m[...], term, preferred_element_type=f32) for term in halves(x))


def from_right(x, m):
    return sum(jnp.dot(term, m[...], preferred_element_type=f32) for term in halves(x))


def lanes(parts):
    return jnp.concatenate(parts, axis=1)


def iota(shape, dim):
    return lax.broadcasted_iota(jnp.int32, shape, dim)


def call(body, outs, args, smem=(), after=(), flops=1_000_000, bytes_accessed=1_000_000):

    def kernel(*refs):
        body(*refs[: len(args)], *refs[len(args) + len(after) :])

    return pl.pallas_call(
        kernel,
        out_shape=[jax.ShapeDtypeStruct(s, d) for s, d in outs],
        in_specs=[
            pl.BlockSpec(memory_space=pltpu.SMEM if i in smem else pltpu.VMEM)
            for i in range(len(args))
        ]
        + [pl.BlockSpec(memory_space=pl.ANY) for _ in after],
        out_specs=[pl.BlockSpec(memory_space=pltpu.VMEM) for _ in outs],
        compiler_params=pltpu.CompilerParams(vmem_limit_bytes=32 * 1024 * 1024),
        cost_estimate=pl.CostEstimate(
            flops=flops, bytes_accessed=bytes_accessed, transcendentals=0
        ),
        name=body.__name__,
    )(*args, *after)


def pair_taps(taps):
    merged = {}
    for b in range(-8, 9):
        for d, w in weight.items():
            merged.setdefault(2 * b + d, []).append(w * taps[1, b + 8])
    return {m: sum(terms[1:], terms[0]) for m, terms in merged.items()}


def fill(gap, values):
    out = jnp.zeros(gap.shape, f32)
    for m, value in values.items():
        out = jnp.where(gap == m, value, out)
    return out


def prep_y(taps, my):
    def gap(rows, first, step):
        column = iota((rows, 76), 1)
        cell = jnp.where(column < 32, column, jnp.where(column < 54, column - 54, column - 22))
        return cell - step * (iota((rows, 76), 0) + first)

    single = {m: taps[0, m + 8] for m in range(-8, 9)}
    part = jnp.concatenate(
        [fill(gap(32, 0, 1), single), fill(gap(24, -1, 2), pair_taps(taps)), fill(gap(8, 0, 4), twice)], axis=0
    )
    first = part.astype(bf16)
    rest = part - first.astype(f32)
    second = rest.astype(bf16)
    third = (rest - second.astype(f32)).astype(bf16)
    my[...] = jnp.concatenate([first.astype(f32), second.astype(f32), third.astype(f32)], axis=0).astype(bf16)


def prep_z(taps, mz1, mz2):
    far_off = 1 << 20

    def z_cells(width):
        row = iota((256, 128), 0)
        cell = jnp.where(row < 128, row, jnp.where(row < 128 + width, row - 128 - width, row - width))
        return jnp.where(row < 128 + 2 * width, cell, far_off)

    single = {m: taps[0, m + 8] for m in range(-8, 9)}
    mz1[...] = fill(z_cells(8) - iota((256, 128), 1), single)
    mz2[...] = fill(z_cells(32) - 2 * (iota((256, 128), 1) - 1), pair_taps(taps))


def toeplitz(profile, shift, size):
    start = pltpu.roll(jnp.broadcast_to(profile, (8, size)), shift, 1)[0:1]
    return pltpu.roll(jnp.broadcast_to(start, (size, size)), 0, 1, stride=1, stride_axis=0)


def prep_top(top_x, top_y, top_z, wz1, wz2, my, wx):
    gx, gy, gz = lax.axis_index("gx"), lax.axis_index("gy"), lax.axis_index("gz")
    tz = toeplitz(top_z[...], lax.rem(258 - 32 * gz, 256), 256)
    lane = iota((256, 256), 1)
    near = jnp.where(lane < 64, tz, 0.0)
    blocks = [near] + [pltpu.roll(near, 64 * a, 1) for a in range(1, 4)]
    for g in range(8):
        for a in range(4):
            rows = pl.ds(128 * g + 32 * a, 32)
            part = blocks[a][32 * g : 32 * g + 32]
            wz1[rows, :], wz2[rows, :] = halves(part)
    ty = toeplitz(lanes([top_y[...]] * 2), lax.rem(130 - 8 * gy, 128), 128)
    my[...] = ty.T[0:16, 0:64]
    tx = toeplitz(lanes([top_x[...]] * 4), lax.rem(130 - 4 * gx, 128), 128)
    spread = jnp.where(iota((32, 2048), 1) // 64 == iota((32, 2048), 0), 1.0, 0.0)
    wx[...] = dot(tx.T[0:16, 0:32], spread)


def odd_place(axis):
    return lax.rem(lax.axis_index(axis), 2) == 1


def choose(is_odd, low, high):
    return jnp.where(is_odd, low, high), jnp.where(is_odd, high, low)


def y_send(own, out_even, out_odd):
    is_odd = odd_place("gy")
    cells = own[...].astype(f32)
    low = jnp.concatenate([cells[i, 0:22] for i in range(16)], axis=0)
    high = jnp.concatenate([cells[i, 10:32] for i in range(16)], axis=0)
    even, odd = choose(is_odd, low, high)
    out_even[...] = even.astype(bf16)
    out_odd[...] = odd.astype(bf16)


def y_step(own, from_odd, from_even, my, n1, n2, q3, out_even, out_odd):
    low, high = arrived("gy", from_even, from_odd, pl.ds(0, 352))
    low, high = low.astype(f32), high.astype(f32)
    cells = own[...].astype(f32)
    columns = lanes([
        jnp.concatenate([cells[i], low[22 * i : 22 * i + 22], high[22 * i : 22 * i + 22]], axis=0)
        for i in range(16)
    ])
    terms = jnp.dot(my[...], columns.astype(bf16), preferred_element_type=f32)
    done = terms[0:64] + (terms[64:128] + terms[128:192])
    parts = [done[:, 128 * i : 128 * i + 128] for i in range(16)]
    parts1 = [part[0:32] for part in parts]
    parts2 = [part[32:56] for part in parts]
    parts3 = [part[56:64] for part in parts]
    for i in range(16):
        n1[i] = parts1[i]
        n2[i] = parts2[i]
        q3[i] = parts3[i]

    def pack(parts, width, high):
        lane = iota(parts[0].shape, 1) // width
        out = jnp.zeros(parts[0].shape, f32)
        for s, part in enumerate(parts):
            shift = (width * s + (width if high else 0)) % 128
            moved = part if shift == 0 else pltpu.roll(part, shift, 1)
            out = jnp.where(lane == s, moved, out)
        return out

    def packed(high):
        groups = [pack(parts1, 8, high)]
        groups += [pack(parts2[4 * g : 4 * g + 4], 32, high) for g in range(4)]
        groups += [pack(parts3[8 * g : 8 * g + 8], 16, high) for g in range(2)]
        return jnp.concatenate(groups, axis=0)

    out_even[...], out_odd[...] = choose(odd_place("gz"), packed(False), packed(True))


def arrived(axis, from_even, from_odd, rows):
    is_odd = odd_place(axis)
    even_part, odd_part = from_even[rows, :], from_odd[rows, :]
    return jnp.where(is_odd, even_part, odd_part), jnp.where(is_odd, odd_part, even_part)


def windows(low, high, slot, width):
    down = (128 - width * slot) % 128
    up = (128 + width - width * slot) % 128
    low = low if down == 0 else pltpu.roll(low, down, 1)
    high = high if up == 0 else pltpu.roll(high, up, 1)
    return jnp.where(iota(low.shape, 1) < width, low, high)


def q3_z_step(q3, from_odd, from_even, mz3, out):
    rows = []
    for g in range(2):
        low, high = arrived("gz", from_even, from_odd, pl.ds(128 + 8 * g, 8))
        rows += [lanes([q3[8 * g + s], windows(low, high, s, 16)]) for s in range(8)]
    full = dot(jnp.concatenate(rows, axis=0), mz3[...])
    slot = iota((8, 128), 1) // 32
    for g in range(4):
        block = full[32 * g : 32 * g + 8]
        for s in range(1, 4):
            block = jnp.where(slot == s, full[32 * g + 8 * s : 32 * g + 8 * s + 8], block)
        out[8 * g : 8 * g + 8] = block


def q3_x_step(low, own, high, out):
    groups = {}
    for first, ref in ((-4, low), (0, own), (4, high)):
        for g in range(4):
            groups[first + g] = ref[8 * g : 8 * g + 8]
    slot = iota((8, 128), 1) // 32
    block = jnp.zeros((8, 128), f32)
    for j in range(4):
        total = jnp.zeros((8, 128), f32)
        for q in range(-3, 3):
            factor = fill(slot, {s: twice.get(4 * q + s, 0.0) for s in range(4)})
            total = total + factor * groups[j + q]
        total = total + pltpu.roll(total, 64, 1)
        total = total + pltpu.roll(total, 32, 1)
        block = jnp.where(slot == j, total, block)
    pair = jnp.concatenate([block, block], axis=0).astype(bf16)
    out[...] = jnp.broadcast_to(pair[None], (32, 16, 128))


def near_z_step(n1, n2, from_odd, from_even, mz1, mz2, n1_out, n2_out, to_low, to_high, to_low2, to_high2):
    low, high = arrived("gz", from_even, from_odd, pl.ds(0, 32))
    rows = jnp.concatenate([lanes([n1[i], windows(low, high, i, 8)]) for i in range(16)], axis=0)
    done1 = dot(rows, mz1[...])
    n1_out[...] = done1.reshape(16, 32, 128)
    rows = []
    for g in range(4):
        low, high = arrived("gz", from_even, from_odd, pl.ds(32 + 24 * g, 24))
        rows += [lanes([n2[4 * g + s], windows(low, high, s, 32)]) for s in range(4)]
    done2 = dot(jnp.concatenate(rows, axis=0), mz2[...])
    to_low[0:256] = done1[0:256]
    to_high[0:256] = done1[256:512]
    for j in range(-1, 10):
        share = jnp.zeros((24, 128), f32)
        for d, w in weight.items():
            if 0 <= 2 * j + d < 16:
                share = share + w * done2[24 * (2 * j + d) : 24 * (2 * j + d) + 24]
        at = 256 + 24 * (j + 1)
        n2_out[j + 1] = share
        to_low[at : at + 24] = share
        to_high[at : at + 24] = share
        if j < 2:
            to_low2[24 * (j + 1) : 24 * (j + 1) + 24] = share
        if j > 6:
            to_high2[24 * (j - 7) : 24 * (j - 7) + 24] = share


def near_x_step(taps, n1, n2, low2, high2, low, high, n1_out, n2_out):
    for t in range(4):
        f = {}
        for i in range(8):
            f[i - 8] = low[32 * i + 8 * t : 32 * i + 8 * t + 8]
            f[i + 16] = high[32 * i + 8 * t : 32 * i + 8 * t + 8]
        for i in range(16):
            f[i] = n1[i, 8 * t : 8 * t + 8]
        for i in range(16):
            total = taps[0, 0] * f[i - 8]
            for a in range(-7, 9):
                total = total + taps[0, a + 8] * f[i + a]
            n1_out[i, 8 * t : 8 * t + 8] = total
    for t in range(3):
        half = {}
        for j in range(-1, 10):
            at = 256 + 24 * (j + 1) + 8 * t
            for place, part in ((j - 8, low[at : at + 8]), (j, n2[j + 1, 8 * t : 8 * t + 8]), (j + 8, high[at : at + 8])):
                half[place] = half[place] + part if place in half else part
        for k in range(3):
            at = 24 * k + 8 * t
            half[k - 9] = half[k - 9] + low2[at : at + 8]
            half[k + 15] = half[k + 15] + high2[at : at + 8]
        for i in range(-1, 10):
            total = taps[1, 0] * half[i - 8]
            for a in range(-7, 9):
                total = total + taps[1, a + 8] * half[i + a]
            n2_out[i + 1, 8 * t : 8 * t + 8] = total


def top_step(gathered, wz1, wz2, my, out):
    whole = gathered[...].astype(f32).reshape(8, 8, 8, 128)
    rows = lanes([whole[:, g].reshape(64, 128) for g in range(8)]).astype(bf16)
    along_z = jnp.dot(rows, wz1[...], preferred_element_type=f32)
    along_z = along_z + jnp.dot(rows, wz2[...], preferred_element_type=f32)
    out[...] = jnp.broadcast_to(dot(my[...], along_z)[None], (8, 16, 256))


def raise_rows(rows, first, last):
    out = {}
    for i in range(first, last + 1):
        if i % 2 == 0:
            out[i] = rows[i // 2]
        else:
            j = (i - 1) // 2
            out[i] = (9.0 / 16.0) * (rows[j] + rows[j + 1]) - (1.0 / 16.0) * (rows[j - 1] + rows[j + 2])
    return out


def last_step(top, wx, n1, n2, y1, z1, y2, z2, out):
    e3 = {}
    for i in range(9):
        total = None
        for g in range(8):
            for h in range(2):
                at = 256 * g + 128 * h
                term = wx[i : i + 1, at : at + 128] * top[g, :, 128 * h : 128 * h + 128]
                total = term if total is None else total + term
        e3[i - 2] = total + pltpu.roll(total, 64, 1)
    e2 = raise_rows(e3, -1, 9)
    wide = from_left(y1, lanes([e2[i] for i in range(-1, 10)]))
    tall = jnp.concatenate([wide[:, 128 * i : 128 * i + 128] for i in range(11)], axis=0)
    tall = from_right(tall, z1) + n2[...].reshape(264, 128)
    tall = from_right(tall, z2)
    wide = from_left(y2, lanes([tall[24 * i : 24 * i + 24] for i in range(11)]))
    rows = raise_rows({i - 1: wide[:, 128 * i : 128 * i + 128] for i in range(11)}, 0, 15)
    for i in range(16):
        out[i] = rows[i] + n1[i]


def per_device(charge, kernel_taps, top_x, top_y, top_z):
    def shift(block, by):
        return lax.ppermute(block, "gx", [(i, (i + by) % 8) for i in range(8)])

    to_even, to_odd = call(y_send, [((352, 128), bf16)] * 2, [charge])
    from_odd = lax.ppermute(to_odd, "gy", swap_odd)
    from_even = lax.ppermute(to_even, "gy", swap_even)
    (my,) = call(prep_y, [((192, 76), bf16)], [kernel_taps], smem=(0,))
    mz1, mz2 = call(prep_z, [((256, 128), f32)] * 2, [kernel_taps], smem=(0,))
    wz1, wz2, ty, wx = call(
        prep_top,
        [((1024, 256), bf16)] * 2 + [((16, 64), f32), ((16, 2048), f32)],
        [top_x[None], top_y[None], top_z[None]],
    )

    n1, n2, q3, to_even, to_odd = call(
        y_step,
        [((16, 32, 128), f32), ((16, 24, 128), f32), ((16, 8, 128), f32), ((144, 128), f32), ((144, 128), f32)],
        [charge, from_odd, from_even, my], after=[mz1, wx],
    )
    from_odd = lax.ppermute(to_odd, "gz", swap_odd)
    from_even = lax.ppermute(to_even, "gz", swap_even)

    (q3,) = call(
        q3_z_step, [((32, 128), f32)],
        [q3, from_odd, from_even, jnp.asarray(z_twice_matrix)],
    )
    (message,) = call(q3_x_step, [((32, 16, 128), bf16)], [shift(q3, 1), q3, shift(q3, -1)])
    gathered = lax.all_to_all(
        message.reshape(64, 8, 128), ("gy", "gz"), split_axis=0, concat_axis=0, tiled=True
    )
    n1, n2, to_low, to_high, to_low2, to_high2 = call(
        near_z_step,
        [((16, 32, 128), f32), ((11, 24, 128), f32)] + [((520, 128), f32)] * 2 + [((72, 128), f32)] * 2,
        [n1, n2, from_odd, from_even, mz1, mz2], after=[message],
    )
    halos = [shift(to_high2, 2), shift(to_low2, -2), shift(to_high, 1), shift(to_low, -1)]
    n1, n2 = call(
        near_x_step, [((16, 32, 128), f32), ((11, 24, 128), f32)],
        [kernel_taps, n1, n2, *halos], smem=(0,),
    )
    (message,) = call(top_step, [((8, 16, 256), f32)], [gathered, wz1, wz2, ty], after=[n1])
    top = lax.all_to_all(message, "gx", split_axis=0, concat_axis=0, tiled=True)
    (result,) = call(
        last_step, [((16, 32, 128), f32)],
        [top, wx, n1, n2, *(jnp.asarray(m, bf16) for m in (y_raise_top, z_raise_top, y_raise, z_raise))],
    )
    return result


def solution(mesh):
    return jax.shard_map(
        per_device,
        mesh=mesh,
        in_specs=(P("gx", "gy", "gz"), P(), P(), P(), P()),
        out_specs=P("gx", "gy", "gz"),
        check_vma=False,
    )
```

```python
import jax
import jax.numpy as jnp
import numpy as np
from jax import lax
from jax.experimental import pallas as pl
from jax.experimental.pallas import tpu as pltpu
from jax.sharding import PartitionSpec as P

f32 = jnp.float32
bf16 = jnp.bfloat16
highest = lax.Precision.HIGHEST
weight = {-3: -1.0 / 16.0, -1: 9.0 / 16.0, 0: 1.0, 1: 9.0 / 16.0, 3: -1.0 / 16.0}

twice = {}
for d0, w0 in weight.items():
    for d1, w1 in weight.items():
        twice[d0 + 2 * d1] = twice.get(d0 + 2 * d1, 0.0) + w0 * w1

swap_even = [(0, 1), (1, 0), (2, 3), (3, 2), (4, 5), (5, 4), (6, 7), (7, 6)]
swap_odd = [(1, 2), (2, 1), (3, 4), (4, 3), (5, 6), (6, 5), (7, 0), (0, 7)]


def table(rows, cols, entry):
    return np.array([[entry(r, c) for c in range(cols)] for r in range(rows)], np.float32)


def restrict(cell, coarse):
    return weight.get(cell - 2 * coarse, 0.0)


z_level2 = [*range(66), -1]
z_top = [*range(35), -2, -1]
z_first = table(128, 128, lambda r, c: restrict(r, z_level2[c]) if c < 67 else 0.0)
z_second = table(128, 128, lambda r, c: restrict(z_level2[r], z_top[c]) if r < 67 and c < 37 else 0.0)


def y_source(row, col):
    coarse = row - 9
    if row >= 35:
        return 0.0
    if col < 32:
        return restrict(col, coarse)
    if col < 40:
        return restrict(col - 40, coarse) if -2 <= coarse <= 1 else 0.0
    if col < 48:
        return restrict(col - 8, coarse) if 15 <= coarse <= 18 else 0.0
    if col < 56:
        return 1.0 if coarse == col - 57 and col < 55 else 0.0
    return 1.0 if coarse == col - 37 and col < 63 else 0.0


y_sources = table(40, 64, y_source)
y_raise_top = table(24, 16, lambda r, c: weight.get((r - 1) - 2 * (c - 2), 0.0) if r < 19 and c < 13 else 0.0)
z_raise_top = table(128, 128, lambda r, c: weight.get((c - 1) - 2 * (r - 2), 0.0) if r < 37 and c < 67 else 0.0)
y_raise = table(32, 24, lambda r, c: weight.get(r - 2 * (c - 1), 0.0) if c < 19 else 0.0)
z_raise = table(128, 128, lambda r, c: weight.get(c - 2 * (r - 1), 0.0) if r < 67 else 0.0)


def dot(a, b):
    return jnp.dot(a, b, precision=highest, preferred_element_type=f32)


def split(x, count):
    terms = []
    for _ in range(count):
        terms.append(x.astype(bf16))
        x = x - terms[-1].astype(f32)
    return terms


def from_left(m, x, count=2):
    return sum(jnp.dot(m[...], term, preferred_element_type=f32) for term in split(x, count))


def from_right(x, m, count=2):
    return sum(jnp.dot(term, m[...], preferred_element_type=f32) for term in split(x, count))


def lanes(parts):
    return jnp.concatenate(parts, axis=1)


def iota(shape, dim):
    return lax.broadcasted_iota(jnp.int32, shape, dim)


def call(body, outs, args, smem=(), after=(), flops=1_000_000, bytes_accessed=1_000_000):

    def kernel(*refs):
        body(*refs[: len(args)], *refs[len(args) + len(after) :])

    return pl.pallas_call(
        kernel,
        out_shape=[jax.ShapeDtypeStruct(s, d) for s, d in outs],
        in_specs=[
            pl.BlockSpec(memory_space=pltpu.SMEM if i in smem else pltpu.VMEM)
            for i in range(len(args))
        ]
        + [pl.BlockSpec(memory_space=pl.ANY) for _ in after],
        out_specs=[pl.BlockSpec(memory_space=pltpu.VMEM) for _ in outs],
        compiler_params=pltpu.CompilerParams(vmem_limit_bytes=32 * 1024 * 1024),
        cost_estimate=pl.CostEstimate(
            flops=flops, bytes_accessed=bytes_accessed, transcendentals=0
        ),
        name=body.__name__,
    )(*args, *after)


def fill(gap, values):
    out = jnp.zeros(gap.shape, f32)
    for m, value in values.items():
        out = jnp.where(gap == m, value, out)
    return out


def prep_y(taps, sources, my1, my2):
    column = iota((32, 48), 1)
    cell = jnp.where(column < 32, column, jnp.where(column < 40, column - 40, column - 8))
    terms = split(fill(cell - iota((32, 48), 0), {m: taps[0, m + 8] for m in range(-8, 9)}), 3)
    my1[...] = jnp.concatenate([term.astype(f32) for term in terms], axis=0).astype(bf16)
    coarse = iota((24, 40), 1) - 9
    near = fill(coarse - (iota((24, 40), 0) - 1), {m: taps[1, m + 8] for m in range(-8, 9)})
    top = fill(iota((8, 40), 1) - 9 - 2 * iota((8, 40), 0), weight)
    my2[...] = dot(jnp.concatenate([near, top], axis=0), sources[...])


def prep_z(taps, mz1, mz2):
    far_off = 1 << 20
    row = iota((256, 128), 0)
    cell = jnp.where(row < 128, row, jnp.where(row < 136, row - 136, row - 8))
    cell = jnp.where(row < 144, cell, far_off)
    mz1[...] = fill(cell - iota((256, 128), 1), {m: taps[0, m + 8] for m in range(-8, 9)})
    own = jnp.where(row < 66, row, jnp.where(row == 66, -1, far_off))
    below = jnp.where(row < 139, row - 137, far_off)
    above = jnp.where(row < 154, row - 80, jnp.where(row == 154, 63, far_off))
    cell = jnp.where(row < 128, own, jnp.where(row < 144, below, above))
    mz2[...] = fill(cell - (iota((256, 128), 1) - 1), {m: taps[1, m + 8] for m in range(-8, 9)})


def toeplitz(profile, shift, size):
    start = pltpu.roll(jnp.broadcast_to(profile, (8, size)), shift, 1)[0:1]
    return pltpu.roll(jnp.broadcast_to(start, (size, size)), 0, 1, stride=1, stride_axis=0)


def prep_top(top_x, top_y, top_z, wz1, wz2, my, wx):
    gx, gy, gz = lax.axis_index("gx"), lax.axis_index("gy"), lax.axis_index("gz")
    tz = toeplitz(top_z[...], lax.rem(258 - 32 * gz, 256), 256)
    lane = iota((256, 256), 1)
    near = jnp.where(lane < 64, tz, 0.0)
    blocks = [near] + [pltpu.roll(near, 64 * a, 1) for a in range(1, 4)]
    for g in range(8):
        for a in range(4):
            rows = pl.ds(128 * g + 32 * a, 32)
            part = blocks[a][32 * g : 32 * g + 32]
            wz1[rows, :], wz2[rows, :] = split(part, 2)
    ty = toeplitz(lanes([top_y[...]] * 2), lax.rem(130 - 8 * gy, 128), 128)
    my[...] = ty.T[0:16, 0:64]
    tx = toeplitz(lanes([top_x[...]] * 4), lax.rem(130 - 4 * gx, 128), 128)
    spread = jnp.where(iota((32, 2048), 1) // 64 == iota((32, 2048), 0), 1.0, 0.0)
    wx[...] = dot(tx.T[0:16, 0:32], spread)


def odd_place(axis):
    return lax.rem(lax.axis_index(axis), 2) == 1


def choose(is_odd, low, high):
    return jnp.where(is_odd, low, high), jnp.where(is_odd, high, low)


def level2_rows(cells):
    return [
        sum(w * cells[2 * j + d] for d, w in weight.items() if 0 <= 2 * j + d < 16) for j in range(-1, 10)
    ]


def y_send(own, out_even, out_odd):
    row, column = iota((16, 32), 0), iota((16, 32), 1)
    y_matrix = fill(column - 2 * jnp.where(row < 8, row + 3, row - 1), weight).astype(bf16)
    row, column = iota((128, 128), 0), iota((128, 128), 1)
    z_matrix = jnp.where(column < 67, fill(row - 2 * jnp.where(column < 66, column, -1), weight), 0.0).astype(bf16)
    cells = own[...].astype(f32)
    wide = from_left(y_matrix, lanes(level2_rows(cells)), 3)
    tall = jnp.concatenate([wide[:, 128 * j : 128 * j + 128] for j in range(11)], axis=0)
    tall = from_right(tall, z_matrix, 3)
    lane = iota((8, 128), 1)

    def message(raw_at, share_at):
        rows, more = [cells[i, raw_at : raw_at + 8] for i in range(16)], jnp.zeros((8, 128), f32)
        for j in range(11):
            part = tall[16 * j + share_at : 16 * j + share_at + 8]
            first = part.astype(bf16).astype(f32)
            second = part - first
            rows.append(jnp.where(lane < 64, first, pltpu.roll(second, 64, 1)))
            beyond = jnp.where(lane % 8 < 4, pltpu.roll(first, (64 + 8 * j) % 128, 1), pltpu.roll(second, (68 + 8 * j) % 128, 1))
            more = jnp.where(lane // 8 == j, beyond, more)
        return jnp.concatenate([*rows, more], axis=0)

    even, odd = choose(odd_place("gy"), message(0, 0), message(24, 8))
    out_even[...] = even.astype(bf16)
    out_odd[...] = odd.astype(bf16)


def own_step(own, z_matrix, out):
    rows = level2_rows(own[...].astype(f32))
    out[...] = from_right(jnp.concatenate(rows, axis=0), z_matrix, 3).reshape(11, 32, 128)


def pack(parts, width, shift):
    slot = iota(parts[0].shape, 1) // width
    out = jnp.zeros(parts[0].shape, f32)
    for s, part in enumerate(parts):
        by = (width * s + shift) % 128
        moved = part if by == 0 else pltpu.roll(part, by, 1)
        out = jnp.where(slot == s, moved, out)
    return out


def y_step(own, from_odd, from_even, own_share, my1, my2, z_matrix, z_next, n1, n2, q3, out_even, out_odd):
    low, high = arrived("gy", from_even, from_odd, pl.ds(0, 224))
    low, high = low.astype(f32), high.astype(f32)
    cells = own[...].astype(f32)
    raw = [[part[8 * i : 8 * i + 8] for i in range(16)] for part in (low, high)]
    columns = lanes([jnp.concatenate([cells[i], raw[0][i], raw[1][i]], axis=0) for i in range(16)])
    terms = jnp.dot(my1[...], columns.astype(bf16), preferred_element_type=f32)
    done = terms[0:32] + (terms[32:64] + terms[64:96])
    parts1 = [done[:, 128 * i : 128 * i + 128] for i in range(16)]

    sides = [level2_rows(part) for part in raw]
    tall = jnp.concatenate([part for j in range(11) for part in (sides[0][j], sides[1][j])], axis=0)
    tall = from_right(tall, z_matrix, 3)
    lane = iota((8, 128), 1)
    columns = []
    for j in range(11):
        stack = [own_share[j], tall[16 * j : 16 * j + 16]]
        for part in (low, high):
            body = part[128 + 8 * j : 136 + 8 * j]
            more = part[216:224] if j == 0 else pltpu.roll(part[216:224], 128 - 8 * j, 1)
            more = pltpu.roll(more + pltpu.roll(more, 124, 1), 64, 1)
            stack.append(jnp.where(lane < 64, body + pltpu.roll(body, 64, 1), jnp.where(lane < 67, more, 0.0)))
        columns.append(jnp.concatenate(stack, axis=0))
    done = dot(my2[...], lanes(columns))
    parts2 = [done[0:24, 128 * j : 128 * j + 128] for j in range(11)]
    half = {j - 1: done[24:32, 128 * j : 128 * j + 128] for j in range(11)}
    rows = [sum(w * half[2 * j + d] for d, w in weight.items() if 2 * j + d in half) for j in range(-2, 7)]
    tall = from_right(jnp.concatenate(rows, axis=0), z_next, 3)
    parts3 = [tall[8 * j : 8 * j + 8] for j in range(9)]
    for i in range(16):
        n1[i] = parts1[i]
    for j in range(11):
        n2[j] = parts2[j]
    for j in range(9):
        q3[j] = parts3[j]

    lane = iota((24, 128), 1)
    edge = [jnp.where(lane < 10, part, pltpu.roll(part, 72, 1)) for part in parts2]
    to_low = [pack(parts1, 8, 0), pack(edge[0:8], 16, 0), pack(edge[8:11], 16, 0), pack(parts3, 8, -35)]
    to_high = [pack(parts1, 8, 8), pack(parts2[0:8], 16, -55), pack(parts2[8:11], 16, -55), pack(parts3, 8, -32)]
    out_even[...], out_odd[...] = choose(
        odd_place("gz"), jnp.concatenate(to_low, axis=0), jnp.concatenate(to_high, axis=0)
    )


def arrived(axis, from_even, from_odd, rows):
    is_odd = odd_place(axis)
    even_part, odd_part = from_even[rows, :], from_odd[rows, :]
    return jnp.where(is_odd, even_part, odd_part), jnp.where(is_odd, odd_part, even_part)


def windows(low, high, slot, width):
    down = (128 - width * slot) % 128
    up = (128 + width - width * slot) % 128
    low = low if down == 0 else pltpu.roll(low, down, 1)
    high = high if up == 0 else pltpu.roll(high, up, 1)
    return jnp.where(iota(low.shape, 1) < width, low, high)


def q3_z_step(q3, from_odd, from_even, out, to_low, to_high):
    low, high = arrived("gz", from_even, from_odd, pl.ds(80, 8))
    lane = iota((8, 128), 1)
    rows = []
    for j in range(9):
        below = low if j == 0 else pltpu.roll(low, 128 - 8 * j, 1)
        above = pltpu.roll(high, (158 - 8 * j) % 128, 1)
        edge = jnp.where(lane < 3, below, jnp.where(lane >= 30, above, 0.0))
        rows.append(jnp.where(lane < 32, q3[j] + edge, 0.0))
    out[...] = pack(rows[2:6], 32, 0)
    to_low[...] = pack([jnp.zeros((8, 128), f32)] * 2 + rows[0:2], 32, 0)
    to_high[...] = pack(rows[6:9], 32, 0)


def q3_x_step(low, own, high, out):
    block = own[...] + low[...] + high[...]
    pair = jnp.concatenate([block, block], axis=0).astype(bf16)
    out[...] = jnp.broadcast_to(pair[None], (32, 16, 128))


def near_z_step(n1, n2, from_odd, from_even, mz1, mz2, n1_out, n2_out, to_low, to_high, to_low2, to_high2):
    low, high = arrived("gz", from_even, from_odd, pl.ds(0, 32))
    rows = jnp.concatenate([lanes([n1[i], windows(low, high, i, 8)]) for i in range(16)], axis=0)
    done1 = dot(rows, mz1[...])
    n1_out[...] = done1.reshape(16, 32, 128)
    rows = []
    for g in range(2):
        low, high = arrived("gz", from_even, from_odd, pl.ds(32 + 24 * g, 24))
        rows += [lanes([n2[j], windows(low, high, j % 8, 16)]) for j in range(8 * g, min(8 * g + 8, 11))]
    done2 = dot(jnp.concatenate(rows, axis=0), mz2[...])
    n2_out[...] = done2.reshape(11, 24, 128)
    to_low[0:256] = done1[0:256]
    to_high[0:256] = done1[256:512]
    to_low[256:520] = done2
    to_high[256:520] = done2
    to_low2[...] = done2[0:72]
    to_high2[...] = done2[192:264]


def near_x_step(taps, n1, n2, low2, high2, low, high, n1_out, n2_out):
    for t in range(4):
        f = {}
        for i in range(8):
            f[i - 8] = low[32 * i + 8 * t : 32 * i + 8 * t + 8]
            f[i + 16] = high[32 * i + 8 * t : 32 * i + 8 * t + 8]
        for i in range(16):
            f[i] = n1[i, 8 * t : 8 * t + 8]
        for i in range(16):
            total = taps[0, 0] * f[i - 8]
            for a in range(-7, 9):
                total = total + taps[0, a + 8] * f[i + a]
            n1_out[i, 8 * t : 8 * t + 8] = total
    for t in range(3):
        half = {}
        for j in range(-1, 10):
            at = 256 + 24 * (j + 1) + 8 * t
            for place, part in ((j - 8, low[at : at + 8]), (j, n2[j + 1, 8 * t : 8 * t + 8]), (j + 8, high[at : at + 8])):
                half[place] = half[place] + part if place in half else part
        for k in range(3):
            at = 24 * k + 8 * t
            half[k - 9] = half[k - 9] + low2[at : at + 8]
            half[k + 15] = half[k + 15] + high2[at : at + 8]
        for i in range(-1, 10):
            total = taps[1, 0] * half[i - 8]
            for a in range(-7, 9):
                total = total + taps[1, a + 8] * half[i + a]
            n2_out[i + 1, 8 * t : 8 * t + 8] = total


def top_step(gathered, wz1, wz2, my, out):
    whole = gathered[...].astype(f32).reshape(8, 8, 8, 128)
    rows = lanes([whole[:, g].reshape(64, 128) for g in range(8)]).astype(bf16)
    along_z = jnp.dot(rows, wz1[...], preferred_element_type=f32)
    along_z = along_z + jnp.dot(rows, wz2[...], preferred_element_type=f32)
    out[...] = jnp.broadcast_to(dot(my[...], along_z)[None], (8, 16, 256))


def raise_rows(rows, first, last):
    out = {}
    for i in range(first, last + 1):
        if i % 2 == 0:
            out[i] = rows[i // 2]
        else:
            j = (i - 1) // 2
            out[i] = (9.0 / 16.0) * (rows[j] + rows[j + 1]) - (1.0 / 16.0) * (rows[j - 1] + rows[j + 2])
    return out


def last_step(top, wx, n1, n2, y1, z1, y2, z2, out):
    e3 = {}
    for i in range(9):
        total = None
        for g in range(8):
            for h in range(2):
                at = 256 * g + 128 * h
                term = wx[i : i + 1, at : at + 128] * top[g, :, 128 * h : 128 * h + 128]
                total = term if total is None else total + term
        e3[i - 2] = total + pltpu.roll(total, 64, 1)
    e2 = raise_rows(e3, -1, 9)
    wide = from_left(y1, lanes([e2[i] for i in range(-1, 10)]))
    tall = jnp.concatenate([wide[:, 128 * i : 128 * i + 128] for i in range(11)], axis=0)
    tall = from_right(tall, z1) + n2[...].reshape(264, 128)
    tall = from_right(tall, z2)
    wide = from_left(y2, lanes([tall[24 * i : 24 * i + 24] for i in range(11)]))
    rows = raise_rows({i - 1: wide[:, 128 * i : 128 * i + 128] for i in range(11)}, 0, 15)
    for i in range(16):
        out[i] = rows[i] + n1[i]


def per_device(charge, kernel_taps, top_x, top_y, top_z):
    def shift(block, by):
        return lax.ppermute(block, "gx", [(i, (i + by) % 8) for i in range(8)])

    z_matrix = jnp.asarray(z_first, bf16)
    to_even, to_odd = call(y_send, [((224, 128), bf16)] * 2, [charge])
    from_odd = lax.ppermute(to_odd, "gy", swap_odd)
    from_even = lax.ppermute(to_even, "gy", swap_even)
    my1, my2 = call(
        prep_y, [((96, 48), bf16), ((32, 64), f32)], [kernel_taps, jnp.asarray(y_sources)], smem=(0,)
    )
    mz1, mz2 = call(prep_z, [((256, 128), f32)] * 2, [kernel_taps], smem=(0,))
    (own_share,) = call(own_step, [((11, 32, 128), f32)], [charge, z_matrix], after=[to_odd])
    wz1, wz2, ty, wx = call(
        prep_top,
        [((1024, 256), bf16)] * 2 + [((16, 64), f32), ((16, 2048), f32)],
        [top_x[None], top_y[None], top_z[None]],
    )

    n1, n2, q3, to_even, to_odd = call(
        y_step,
        [((16, 32, 128), f32), ((11, 24, 128), f32), ((9, 8, 128), f32), ((88, 128), f32), ((88, 128), f32)],
        [charge, from_odd, from_even, own_share, my1, my2, z_matrix, jnp.asarray(z_second, bf16)],
        after=[mz1, wx],
    )
    from_odd = lax.ppermute(to_odd, "gz", swap_odd)
    from_even = lax.ppermute(to_even, "gz", swap_even)

    q3, to_low, to_high = call(q3_z_step, [((8, 128), f32)] * 3, [q3, from_odd, from_even])
    (message,) = call(q3_x_step, [((32, 16, 128), bf16)], [shift(to_high, 1), q3, shift(to_low, -1)])
    gathered = lax.all_to_all(
        message.reshape(64, 8, 128), ("gy", "gz"), split_axis=0, concat_axis=0, tiled=True
    )
    n1, n2, to_low, to_high, to_low2, to_high2 = call(
        near_z_step,
        [((16, 32, 128), f32), ((11, 24, 128), f32)] + [((520, 128), f32)] * 2 + [((72, 128), f32)] * 2,
        [n1, n2, from_odd, from_even, mz1, mz2], after=[message],
    )
    halos = [shift(to_high2, 2), shift(to_low2, -2), shift(to_high, 1), shift(to_low, -1)]
    n1, n2 = call(
        near_x_step, [((16, 32, 128), f32), ((11, 24, 128), f32)],
        [kernel_taps, n1, n2, *halos], smem=(0,),
    )
    (message,) = call(top_step, [((8, 16, 256), f32)], [gathered, wz1, wz2, ty], after=[n1])
    top = lax.all_to_all(message, "gx", split_axis=0, concat_axis=0, tiled=True)
    (result,) = call(
        last_step, [((16, 32, 128), f32)],
        [top, wx, n1, n2, *(jnp.asarray(m, bf16) for m in (y_raise_top, z_raise_top, y_raise, z_raise))],
    )
    return result


def solution(mesh):
    return jax.shard_map(
        per_device,
        mesh=mesh,
        in_specs=(P("gx", "gy", "gz"), P(), P(), P(), P()),
        out_specs=P("gx", "gy", "gz"),
        check_vma=False,
    )
```

```python
import jax
import jax.numpy as jnp
import numpy as np
from jax import lax
from jax.experimental import pallas as pl
from jax.experimental.pallas import tpu as pltpu
from jax.sharding import PartitionSpec as P

f32 = jnp.float32
bf16 = jnp.bfloat16
highest = lax.Precision.HIGHEST
weight = {-3: -1.0 / 16.0, -1: 9.0 / 16.0, 0: 1.0, 1: 9.0 / 16.0, 3: -1.0 / 16.0}

twice = {}
for d0, w0 in weight.items():
    for d1, w1 in weight.items():
        twice[d0 + 2 * d1] = twice.get(d0 + 2 * d1, 0.0) + w0 * w1

swap_even = [(0, 1), (1, 0), (2, 3), (3, 2), (4, 5), (5, 4), (6, 7), (7, 6)]
swap_odd = [(1, 2), (2, 1), (3, 4), (4, 3), (5, 6), (6, 5), (7, 0), (0, 7)]


def table(rows, cols, entry):
    return np.array([[entry(r, c) for c in range(cols)] for r in range(rows)], np.float32)


def restrict(cell, coarse):
    return weight.get(cell - 2 * coarse, 0.0)


z_level2 = [*range(66), -1]
z_top = [*range(35), -2, -1]
z_first = table(128, 128, lambda r, c: restrict(r, z_level2[c]) if c < 67 else 0.0)
z_second = table(128, 128, lambda r, c: restrict(z_level2[r], z_top[c]) if r < 67 and c < 37 else 0.0)


def y_source(row, col):
    coarse = row - 9
    if row >= 35:
        return 0.0
    if col < 32:
        return restrict(col, coarse)
    if col < 40:
        return restrict(col - 40, coarse) if -2 <= coarse <= 1 else 0.0
    if col < 48:
        return restrict(col - 8, coarse) if 15 <= coarse <= 18 else 0.0
    if col < 56:
        return 1.0 if coarse == col - 57 and col < 55 else 0.0
    return 1.0 if coarse == col - 37 and col < 63 else 0.0


y_sources = table(40, 64, y_source)
y_raise_top = table(24, 16, lambda r, c: weight.get((r - 1) - 2 * (c - 2), 0.0) if r < 19 and c < 13 else 0.0)
z_raise_top = table(
    128,
    128,
    lambda r, c: weight.get((c - 1) - 2 * ((r if r < 32 else 32 + (r - 32) % 5) - 2), 0.0) if r < 57 and c < 67 else 0.0,
)
y_raise = table(32, 24, lambda r, c: weight.get(r - 2 * (c - 1), 0.0) if c < 19 else 0.0)
z_raise = table(128, 128, lambda r, c: weight.get(c - 2 * (r - 1), 0.0) if r < 67 else 0.0)


def dot(a, b):
    return jnp.dot(a, b, precision=highest, preferred_element_type=f32)


def split(x, count):
    terms = []
    for _ in range(count):
        terms.append(x.astype(bf16))
        x = x - terms[-1].astype(f32)
    return terms


def from_left(m, x, count=2):
    return sum(jnp.dot(m[...], term, preferred_element_type=f32) for term in split(x, count))


def from_right(x, m, count=2):
    return sum(jnp.dot(term, m[...], preferred_element_type=f32) for term in split(x, count))


def lanes(parts):
    return jnp.concatenate(parts, axis=1)


def iota(shape, dim):
    return lax.broadcasted_iota(jnp.int32, shape, dim)


def call(body, outs, args, smem=(), after=(), flops=1_000_000, bytes_accessed=1_000_000):

    def kernel(*refs):
        body(*refs[: len(args)], *refs[len(args) + len(after) :])

    return pl.pallas_call(
        kernel,
        out_shape=[jax.ShapeDtypeStruct(s, d) for s, d in outs],
        in_specs=[
            pl.BlockSpec(memory_space=pltpu.SMEM if i in smem else pltpu.VMEM)
            for i in range(len(args))
        ]
        + [pl.BlockSpec(memory_space=pl.ANY) for _ in after],
        out_specs=[pl.BlockSpec(memory_space=pltpu.VMEM) for _ in outs],
        compiler_params=pltpu.CompilerParams(vmem_limit_bytes=32 * 1024 * 1024),
        cost_estimate=pl.CostEstimate(
            flops=flops, bytes_accessed=bytes_accessed, transcendentals=0
        ),
        name=body.__name__,
    )(*args, *after)


def fill(gap, values):
    out = jnp.zeros(gap.shape, f32)
    for m, value in values.items():
        out = jnp.where(gap == m, value, out)
    return out


def prep_y(taps, sources, my1, my2):
    column = iota((32, 48), 1)
    cell = jnp.where(column < 32, column, jnp.where(column < 40, column - 40, column - 8))
    terms = split(fill(cell - iota((32, 48), 0), {m: taps[0, m + 8] for m in range(-8, 9)}), 2)
    my1[...] = jnp.concatenate([term.astype(f32) for term in terms], axis=0).astype(bf16)
    coarse = iota((24, 40), 1) - 9
    near = fill(coarse - (iota((24, 40), 0) - 1), {m: taps[1, m + 8] for m in range(-8, 9)})
    top = fill(iota((8, 40), 1) - 9 - 2 * iota((8, 40), 0), weight)
    my2[...] = dot(jnp.concatenate([near, top], axis=0), sources[...])


def prep_z(taps, mz1, mz2):
    far_off = 1 << 20
    row = iota((256, 128), 0)
    cell = jnp.where(row < 128, row, jnp.where(row < 136, row - 136, row - 8))
    cell = jnp.where(row < 144, cell, far_off)
    mz1[...] = fill(cell - iota((256, 128), 1), {m: taps[0, m + 8] for m in range(-8, 9)})
    own = jnp.where(row < 66, row, jnp.where(row == 66, -1, far_off))
    below = jnp.where(row < 139, row - 137, far_off)
    above = jnp.where(row < 154, row - 80, jnp.where(row == 154, 63, far_off))
    cell = jnp.where(row < 128, own, jnp.where(row < 144, below, above))
    mz2[...] = fill(cell - (iota((256, 128), 1) - 1), {m: taps[1, m + 8] for m in range(-8, 9)})


def toeplitz(profile, shift, size):
    start = pltpu.roll(jnp.broadcast_to(profile, (8, size)), shift, 1)[0:1]
    return pltpu.roll(jnp.broadcast_to(start, (size, size)), 0, 1, stride=1, stride_axis=0)


def prep_top(top_x, top_y, top_z, wz1, wz2, my, wx):
    gx, gy, gz = lax.axis_index("gx"), lax.axis_index("gy"), lax.axis_index("gz")
    tz = toeplitz(top_z[...], lax.rem(258 - 32 * gz, 256), 256)
    lane = iota((256, 128), 1)
    near, past = tz[:, 0:128], jnp.zeros((256, 128), f32)
    for t in range(5):
        past = jnp.where(lane // 5 == t, pltpu.roll(near, 96 + 5 * t, 1), past)
    near, past = jnp.where(lane < 32, near, 0.0), jnp.where(lane < 25, past, 0.0)
    for a in range(4):
        both = lanes([pltpu.roll(part, 32 * a, 1) if a else part for part in (near, past)])
        for g in range(8):
            rows = pl.ds(128 * g + 32 * a, 32)
            wz1[rows, :], wz2[rows, :] = split(both[32 * g : 32 * g + 32], 2)
    ty = toeplitz(lanes([top_y[...]] * 2), lax.rem(130 - 8 * gy, 128), 128)
    my[...] = ty.T[0:16, 0:64]
    tx = toeplitz(lanes([top_x[...]] * 4), lax.rem(130 - 4 * gx, 128), 128)
    spread = jnp.where(iota((32, 1024), 1) // 32 == iota((32, 1024), 0), 1.0, 0.0)
    wx[...] = dot(tx.T[0:16, 0:32], spread)


def odd_place(axis):
    return lax.rem(lax.axis_index(axis), 2) == 1


def choose(is_odd, low, high):
    return jnp.where(is_odd, low, high), jnp.where(is_odd, high, low)


def level2_rows(cells):
    return [
        sum(w * cells[2 * j + d] for d, w in weight.items() if 0 <= 2 * j + d < 16) for j in range(-1, 10)
    ]


def y_send(own, out_even, out_odd):
    row, column = iota((16, 32), 0), iota((16, 32), 1)
    y_matrix = fill(column - 2 * jnp.where(row < 8, row + 3, row - 1), weight).astype(bf16)
    row, column = iota((128, 128), 0), iota((128, 128), 1)
    z_matrix = jnp.where(column < 67, fill(row - 2 * jnp.where(column < 66, column, -1), weight), 0.0).astype(bf16)
    cells = own[...].astype(f32)
    wide = from_left(y_matrix, lanes(level2_rows(cells)), 3)
    tall = jnp.concatenate([wide[:, 128 * j : 128 * j + 128] for j in range(11)], axis=0)
    tall = from_right(tall, z_matrix, 3)
    lane = iota((8, 128), 1)

    def message(raw_at, share_at):
        rows, more = [cells[i, raw_at : raw_at + 8] for i in range(16)], jnp.zeros((8, 128), f32)
        for j in range(11):
            part = tall[16 * j + share_at : 16 * j + share_at + 8]
            first = part.astype(bf16).astype(f32)
            second = part - first
            rows.append(jnp.where(lane < 64, first, pltpu.roll(second, 64, 1)))
            beyond = jnp.where(lane % 8 < 4, pltpu.roll(first, (64 + 8 * j) % 128, 1), pltpu.roll(second, (68 + 8 * j) % 128, 1))
            more = jnp.where(lane // 8 == j, beyond, more)
        return jnp.concatenate([*rows, more], axis=0)

    even, odd = choose(odd_place("gy"), message(0, 0), message(24, 8))
    out_even[...] = even.astype(bf16)
    out_odd[...] = odd.astype(bf16)


def own_step(own, z_matrix, out):
    rows = level2_rows(own[...].astype(f32))
    out[...] = from_right(jnp.concatenate(rows, axis=0), z_matrix, 3).reshape(11, 32, 128)


def pack(parts, width, shift):
    slot = iota(parts[0].shape, 1) // width
    out = jnp.zeros(parts[0].shape, f32)
    for s, part in enumerate(parts):
        by = (width * s + shift) % 128
        moved = part if by == 0 else pltpu.roll(part, by, 1)
        out = jnp.where(slot == s, moved, out)
    return out


def y_step(own, from_odd, from_even, own_share, my1, my2, z_matrix, z_next, n1, n2, q3, out_even, out_odd):
    low, high = arrived("gy", from_even, from_odd, pl.ds(0, 224))
    low, high = low.astype(f32), high.astype(f32)
    cells = own[...].astype(f32)
    raw = [[part[8 * i : 8 * i + 8] for i in range(16)] for part in (low, high)]
    columns = lanes([jnp.concatenate([cells[i], raw[0][i], raw[1][i]], axis=0) for i in range(16)])
    terms = jnp.dot(my1[...], columns.astype(bf16), preferred_element_type=f32)
    done = terms[0:32] + terms[32:64]
    parts1 = [done[:, 128 * i : 128 * i + 128] for i in range(16)]

    sides = [level2_rows(part) for part in raw]
    tall = jnp.concatenate([part for j in range(11) for part in (sides[0][j], sides[1][j])], axis=0)
    tall = from_right(tall, z_matrix, 3)
    lane = iota((8, 128), 1)
    columns = []
    for j in range(11):
        stack = [own_share[j], tall[16 * j : 16 * j + 16]]
        for part in (low, high):
            body = part[128 + 8 * j : 136 + 8 * j]
            more = part[216:224] if j == 0 else pltpu.roll(part[216:224], 128 - 8 * j, 1)
            more = pltpu.roll(more + pltpu.roll(more, 124, 1), 64, 1)
            stack.append(jnp.where(lane < 64, body + pltpu.roll(body, 64, 1), jnp.where(lane < 67, more, 0.0)))
        columns.append(jnp.concatenate(stack, axis=0))
    done = dot(my2[...], lanes(columns))
    parts2 = [done[0:24, 128 * j : 128 * j + 128] for j in range(11)]
    half = {j - 1: done[24:32, 128 * j : 128 * j + 128] for j in range(11)}
    rows = [sum(w * half[2 * j + d] for d, w in weight.items() if 2 * j + d in half) for j in range(-2, 7)]
    tall = from_right(jnp.concatenate(rows, axis=0), z_next, 3)
    parts3 = [tall[8 * j : 8 * j + 8] for j in range(9)]
    for i in range(16):
        n1[i] = parts1[i]
    for j in range(11):
        n2[j] = parts2[j]
    for j in range(9):
        q3[j] = parts3[j]

    lane = iota((24, 128), 1)
    edge = [jnp.where(lane < 10, part, pltpu.roll(part, 72, 1)) for part in parts2]
    to_low = [pack(parts1, 8, 0), pack(edge[0:8], 16, 0), pack(edge[8:11], 16, 0), pack(parts3, 8, -35)]
    to_high = [pack(parts1, 8, 8), pack(parts2[0:8], 16, -55), pack(parts2[8:11], 16, -55), pack(parts3, 8, -32)]
    out_even[...], out_odd[...] = choose(
        odd_place("gz"), jnp.concatenate(to_low, axis=0), jnp.concatenate(to_high, axis=0)
    )


def arrived(axis, from_even, from_odd, rows):
    is_odd = odd_place(axis)
    even_part, odd_part = from_even[rows, :], from_odd[rows, :]
    return jnp.where(is_odd, even_part, odd_part), jnp.where(is_odd, odd_part, even_part)


def windows(low, high, slot, width):
    down = (128 - width * slot) % 128
    up = (128 + width - width * slot) % 128
    low = low if down == 0 else pltpu.roll(low, down, 1)
    high = high if up == 0 else pltpu.roll(high, up, 1)
    return jnp.where(iota(low.shape, 1) < width, low, high)


def q3_z_step(q3, from_odd, from_even, out, to_low, to_high):
    low, high = arrived("gz", from_even, from_odd, pl.ds(80, 8))
    lane = iota((8, 128), 1)
    rows = []
    for j in range(9):
        below = low if j == 0 else pltpu.roll(low, 128 - 8 * j, 1)
        above = pltpu.roll(high, (158 - 8 * j) % 128, 1)
        edge = jnp.where(lane < 3, below, jnp.where(lane >= 30, above, 0.0))
        rows.append(jnp.where(lane < 32, q3[j] + edge, 0.0))
    out[...] = pack(rows[2:6], 32, 0)
    to_low[...] = pack([jnp.zeros((8, 128), f32)] * 2 + rows[0:2], 32, 0)
    to_high[...] = pack(rows[6:9], 32, 0)


def q3_x_step(low, own, high, out):
    block = own[...] + low[...] + high[...]
    pair = jnp.concatenate([block, block], axis=0).astype(bf16)
    out[...] = jnp.broadcast_to(pair[None], (32, 16, 128))


def near_z_step(n1, n2, from_odd, from_even, mz1, mz2, n1_out, n2_out, to_low, to_high, to_even, to_odd):
    low, high = arrived("gz", from_even, from_odd, pl.ds(0, 32))
    rows = jnp.concatenate([lanes([n1[i], windows(low, high, i, 8)]) for i in range(16)], axis=0)
    done1 = dot(rows, mz1[...])
    n1_out[...] = done1.reshape(16, 32, 128)
    rows = []
    for g in range(2):
        low, high = arrived("gz", from_even, from_odd, pl.ds(32 + 24 * g, 24))
        rows += [lanes([n2[j], windows(low, high, j % 8, 16)]) for j in range(8 * g, min(8 * g + 8, 11))]
    done2 = dot(jnp.concatenate(rows, axis=0), mz2[...])
    n2_out[...] = done2.reshape(11, 24, 128)
    to_low[0:256] = done1[0:256]
    to_high[0:256] = done1[256:512]
    to_low[256:520] = done2
    to_high[256:520] = done2
    odd_chip = lax.rem(lax.axis_index("gx") // 2, 2) == 1
    to_even[...], to_odd[...] = choose(odd_chip, done2[0:72], done2[192:264])


def near_x_step(taps, n1, n2, even2, odd2, low, high, n1_out, n2_out):
    odd_chip = lax.rem(lax.axis_index("gx") // 2, 2) == 1
    low2 = jnp.where(odd_chip, even2[...], odd2[...])
    high2 = jnp.where(odd_chip, odd2[...], even2[...])
    for t in range(4):
        f = {}
        for i in range(8):
            f[i - 8] = low[32 * i + 8 * t : 32 * i + 8 * t + 8]
            f[i + 16] = high[32 * i + 8 * t : 32 * i + 8 * t + 8]
        for i in range(16):
            f[i] = n1[i, 8 * t : 8 * t + 8]
        for i in range(16):
            total = taps[0, 0] * f[i - 8]
            for a in range(-7, 9):
                total = total + taps[0, a + 8] * f[i + a]
            n1_out[i, 8 * t : 8 * t + 8] = total
    for t in range(3):
        half = {}
        for j in range(-1, 10):
            at = 256 + 24 * (j + 1) + 8 * t
            for place, part in ((j - 8, low[at : at + 8]), (j, n2[j + 1, 8 * t : 8 * t + 8]), (j + 8, high[at : at + 8])):
                half[place] = half[place] + part if place in half else part
        for k in range(3):
            at = 24 * k + 8 * t
            half[k - 9] = half[k - 9] + low2[at : at + 8]
            half[k + 15] = half[k + 15] + high2[at : at + 8]
        for i in range(-1, 10):
            total = taps[1, 0] * half[i - 8]
            for a in range(-7, 9):
                total = total + taps[1, a + 8] * half[i + a]
            n2_out[i + 1, 8 * t : 8 * t + 8] = total


def top_step(gathered, wz1, wz2, my, out):
    whole = gathered[...].astype(f32).reshape(8, 8, 8, 128)
    rows = lanes([whole[:, g].reshape(64, 128) for g in range(8)]).astype(bf16)
    along_z = jnp.dot(rows, wz1[...], preferred_element_type=f32)
    along_z = along_z + jnp.dot(rows, wz2[...], preferred_element_type=f32)
    done = dot(my[...], along_z)
    row = iota((16, 128), 0)
    block, past = done[:, 0:128], jnp.where(iota((16, 128), 1) % 32 // 5 == row % 5, done[:, 128:256], 0.0)
    for t in range(3):
        mine = (row // 5 == t) & (row < 13)
        block = jnp.where(row == 13 + t, jnp.sum(jnp.where(mine, past, 0.0), axis=0, keepdims=True), block)
    out[...] = jnp.broadcast_to(block[None], (8, 16, 128))


def raise_rows(rows, first, last):
    out = {}
    for i in range(first, last + 1):
        if i % 2 == 0:
            out[i] = rows[i // 2]
        else:
            j = (i - 1) // 2
            out[i] = (9.0 / 16.0) * (rows[j] + rows[j + 1]) - (1.0 / 16.0) * (rows[j - 1] + rows[j + 2])
    return out


def last_step(top, wx, n1, n2, y1, z1, y2, z2, out):
    e3 = {}
    row, lane = iota((16, 128), 0), iota((16, 128), 1)
    here = (lane >= 32) & (lane < 57) & (lane % 32 // 5 == row % 5)
    for i in range(9):
        total = None
        for g in range(8):
            term = wx[i : i + 1, 128 * g : 128 * g + 128] * top[g]
            total = term if total is None else total + term
        total = total + pltpu.roll(total, 64, 1)
        total = total + pltpu.roll(total, 32, 1)
        past = jnp.where(row < 5, total[13:14], jnp.where(row < 10, total[14:15], total[15:16]))
        e3[i - 2] = jnp.where(lane < 32, total, jnp.where(here, past, 0.0))
    e2 = raise_rows(e3, -1, 9)
    wide = from_left(y1, lanes([e2[i] for i in range(-1, 10)]))
    tall = jnp.concatenate([wide[:, 128 * i : 128 * i + 128] for i in range(11)], axis=0)
    tall = from_right(tall, z1) + n2[...].reshape(264, 128)
    tall = from_right(tall, z2)
    wide = from_left(y2, lanes([tall[24 * i : 24 * i + 24] for i in range(11)]))
    rows = raise_rows({i - 1: wide[:, 128 * i : 128 * i + 128] for i in range(11)}, 0, 15)
    for i in range(16):
        out[i] = rows[i] + n1[i]


def per_device(charge, kernel_taps, top_x, top_y, top_z):
    def shift(block, by):
        return lax.ppermute(block, "gx", [(i, (i + by) % 8) for i in range(8)])

    z_matrix = jnp.asarray(z_first, bf16)
    to_even, to_odd = call(y_send, [((224, 128), bf16)] * 2, [charge])
    from_odd = lax.ppermute(to_odd, "gy", swap_odd)
    from_even = lax.ppermute(to_even, "gy", swap_even)
    my1, my2 = call(
        prep_y, [((64, 48), bf16), ((32, 64), f32)], [kernel_taps, jnp.asarray(y_sources)], smem=(0,)
    )
    mz1, mz2 = call(prep_z, [((256, 128), f32)] * 2, [kernel_taps], smem=(0,))
    (own_share,) = call(own_step, [((11, 32, 128), f32)], [charge, z_matrix], after=[to_odd])
    wz1, wz2, ty, wx = call(
        prep_top,
        [((1024, 256), bf16)] * 2 + [((16, 64), f32), ((16, 1024), f32)],
        [top_x[None], top_y[None], top_z[None]],
    )

    n1, n2, q3, to_even, to_odd = call(
        y_step,
        [((16, 32, 128), f32), ((11, 24, 128), f32), ((9, 8, 128), f32), ((88, 128), f32), ((88, 128), f32)],
        [charge, from_odd, from_even, own_share, my1, my2, z_matrix, jnp.asarray(z_second, bf16)],
        after=[mz1, wx],
    )
    from_odd = lax.ppermute(to_odd, "gz", swap_odd)
    from_even = lax.ppermute(to_even, "gz", swap_even)

    q3, to_low, to_high = call(q3_z_step, [((8, 128), f32)] * 3, [q3, from_odd, from_even])
    (message,) = call(q3_x_step, [((32, 16, 128), bf16)], [shift(to_high, 1), q3, shift(to_low, -1)])
    gathered = lax.all_to_all(
        message.reshape(64, 8, 128), ("gy", "gz"), split_axis=0, concat_axis=0, tiled=True
    )
    n1, n2, to_low, to_high, to_even, to_odd = call(
        near_z_step,
        [((16, 32, 128), f32), ((11, 24, 128), f32)] + [((520, 128), f32)] * 2 + [((72, 128), f32)] * 2,
        [n1, n2, from_odd, from_even, mz1, mz2], after=[message],
    )
    halos = [
        lax.ppermute(to_even, "gx", [(0, 2), (2, 0), (1, 3), (3, 1), (4, 6), (6, 4), (5, 7), (7, 5)]),
        lax.ppermute(to_odd, "gx", [(2, 4), (4, 2), (3, 5), (5, 3), (6, 0), (0, 6), (7, 1), (1, 7)]),
        shift(to_high, 1),
        shift(to_low, -1),
    ]
    n1, n2 = call(
        near_x_step, [((16, 32, 128), f32), ((11, 24, 128), f32)],
        [kernel_taps, n1, n2, *halos], smem=(0,),
    )
    (message,) = call(top_step, [((8, 16, 128), f32)], [gathered, wz1, wz2, ty], after=[n1])
    top = lax.all_to_all(message, "gx", split_axis=0, concat_axis=0, tiled=True)
    (result,) = call(
        last_step, [((16, 32, 128), f32)],
        [top, wx, n1, n2, *(jnp.asarray(m, bf16) for m in (y_raise_top, z_raise_top, y_raise, z_raise))],
    )
    return result


def solution(mesh):
    return jax.shard_map(
        per_device,
        mesh=mesh,
        in_specs=(P("gx", "gy", "gz"), P(), P(), P(), P()),
        out_specs=P("gx", "gy", "gz"),
        check_vma=False,
    )
```

```python
import jax
import jax.numpy as jnp
import numpy as np
from jax import lax
from jax.experimental import pallas as pl
from jax.experimental.pallas import tpu as pltpu
from jax.sharding import PartitionSpec as P

f32 = jnp.float32
bf16 = jnp.bfloat16
highest = lax.Precision.HIGHEST
weight = {-3: -1.0 / 16.0, -1: 9.0 / 16.0, 0: 1.0, 1: 9.0 / 16.0, 3: -1.0 / 16.0}

twice = {}
for d0, w0 in weight.items():
    for d1, w1 in weight.items():
        twice[d0 + 2 * d1] = twice.get(d0 + 2 * d1, 0.0) + w0 * w1

swap_even = [(0, 1), (1, 0), (2, 3), (3, 2), (4, 5), (5, 4), (6, 7), (7, 6)]
swap_odd = [(1, 2), (2, 1), (3, 4), (4, 3), (5, 6), (6, 5), (7, 0), (0, 7)]


def table(rows, cols, entry):
    return np.array([[entry(r, c) for c in range(cols)] for r in range(rows)], np.float32)


def restrict(cell, coarse):
    return weight.get(cell - 2 * coarse, 0.0)


z_level2 = [*range(66), -1]
z_top = [*range(35), -2, -1]
z_first = table(128, 128, lambda r, c: restrict(r, z_level2[c]) if c < 67 else 0.0)
z_second = table(128, 128, lambda r, c: restrict(z_level2[r], z_top[c]) if r < 67 and c < 37 else 0.0)


def y_source(row, col):
    coarse = row - 9
    if row >= 35:
        return 0.0
    if col < 32:
        return restrict(col, coarse)
    if col < 40:
        return restrict(col - 40, coarse) if -2 <= coarse <= 1 else 0.0
    if col < 48:
        return restrict(col - 8, coarse) if 15 <= coarse <= 18 else 0.0
    if col < 56:
        return 1.0 if coarse == col - 57 and col < 55 else 0.0
    return 1.0 if coarse == col - 37 and col < 63 else 0.0


y_sources = table(40, 64, y_source)
y_raise_top = table(24, 16, lambda r, c: weight.get((r - 1) - 2 * (c - 2), 0.0) if r < 19 and c < 13 else 0.0)
z_raise_top = table(
    128,
    128,
    lambda r, c: weight.get((c - 1) - 2 * ((r if r < 32 else 32 + (r - 32) % 5) - 2), 0.0) if r < 57 and c < 67 else 0.0,
)
y_raise = table(32, 24, lambda r, c: weight.get(r - 2 * (c - 1), 0.0) if c < 19 else 0.0)
z_raise = table(128, 128, lambda r, c: weight.get(c - 2 * (r - 1), 0.0) if r < 67 else 0.0)


def dot(a, b):
    return jnp.dot(a, b, precision=highest, preferred_element_type=f32)


def split(x, count):
    terms = []
    for _ in range(count):
        terms.append(x.astype(bf16))
        x = x - terms[-1].astype(f32)
    return terms


def from_left(m, x, count=2):
    return sum(jnp.dot(m[...], term, preferred_element_type=f32) for term in split(x, count))


def from_right(x, m, count=2):
    return sum(jnp.dot(term, m[...], preferred_element_type=f32) for term in split(x, count))


def lanes(parts):
    return jnp.concatenate(parts, axis=1)


def iota(shape, dim):
    return lax.broadcasted_iota(jnp.int32, shape, dim)


def call(body, outs, args, smem=(), after=(), flops=1_000_000, bytes_accessed=1_000_000):

    def kernel(*refs):
        body(*refs[: len(args)], *refs[len(args) + len(after) :])

    return pl.pallas_call(
        kernel,
        out_shape=[jax.ShapeDtypeStruct(s, d) for s, d in outs],
        in_specs=[
            pl.BlockSpec(memory_space=pltpu.SMEM if i in smem else pltpu.VMEM)
            for i in range(len(args))
        ]
        + [pl.BlockSpec(memory_space=pl.ANY) for _ in after],
        out_specs=[pl.BlockSpec(memory_space=pltpu.VMEM) for _ in outs],
        compiler_params=pltpu.CompilerParams(vmem_limit_bytes=32 * 1024 * 1024),
        cost_estimate=pl.CostEstimate(
            flops=flops, bytes_accessed=bytes_accessed, transcendentals=0
        ),
        name=body.__name__,
    )(*args, *after)


def fill(gap, values):
    out = jnp.zeros(gap.shape, f32)
    for m, value in values.items():
        out = jnp.where(gap == m, value, out)
    return out


def prep_y(taps, sources, my1, my2):
    column = iota((32, 48), 1)
    cell = jnp.where(column < 32, column, jnp.where(column < 40, column - 40, column - 8))
    terms = split(fill(cell - iota((32, 48), 0), {m: taps[0, m + 8] for m in range(-8, 9)}), 2)
    my1[...] = jnp.concatenate([term.astype(f32) for term in terms], axis=0).astype(bf16)
    coarse = iota((24, 40), 1) - 9
    near = fill(coarse - (iota((24, 40), 0) - 1), {m: taps[1, m + 8] for m in range(-8, 9)})
    top = fill(iota((8, 40), 1) - 9 - 2 * iota((8, 40), 0), weight)
    my2[...] = dot(jnp.concatenate([near, top], axis=0), sources[...])


def prep_z(taps, mz1, mz2):
    far_off = 1 << 20
    row = iota((256, 128), 0)
    cell = jnp.where(row < 128, row, jnp.where(row < 136, row - 136, row - 8))
    cell = jnp.where(row < 144, cell, far_off)
    mz1[...] = fill(cell - iota((256, 128), 1), {m: taps[0, m + 8] for m in range(-8, 9)})
    own = jnp.where(row < 66, row, jnp.where(row == 66, -1, far_off))
    below = jnp.where(row < 139, row - 137, far_off)
    above = jnp.where(row < 154, row - 80, jnp.where(row == 154, 63, far_off))
    cell = jnp.where(row < 128, own, jnp.where(row < 144, below, above))
    mz2[...] = fill(cell - (iota((256, 128), 1) - 1), {m: taps[1, m + 8] for m in range(-8, 9)})


def toeplitz(profile, shift, size):
    start = pltpu.roll(jnp.broadcast_to(profile, (8, size)), shift, 1)[0:1]
    return pltpu.roll(jnp.broadcast_to(start, (size, size)), 0, 1, stride=1, stride_axis=0)


def prep_top(top_x, top_y, top_z, wz1, wz2, my, wx):
    gx, gy, gz = lax.axis_index("gx"), lax.axis_index("gy"), lax.axis_index("gz")
    tz = toeplitz(top_z[...], lax.rem(258 - 32 * gz, 256), 256)
    lane = iota((256, 128), 1)
    near, past = tz[:, 0:128], jnp.zeros((256, 128), f32)
    for t in range(5):
        past = jnp.where(lane // 5 == t, pltpu.roll(near, 96 + 5 * t, 1), past)
    near, past = jnp.where(lane < 32, near, 0.0), jnp.where(lane < 25, past, 0.0)
    for a in range(4):
        both = lanes([pltpu.roll(part, 32 * a, 1) if a else part for part in (near, past)])
        for g in range(8):
            rows = pl.ds(128 * g + 32 * a, 32)
            wz1[rows, :], wz2[rows, :] = split(both[32 * g : 32 * g + 32], 2)
    ty = toeplitz(lanes([top_y[...]] * 2), lax.rem(130 - 8 * gy, 128), 128)
    my[...] = ty.T[0:16, 0:64]
    tx = toeplitz(lanes([top_x[...]] * 4), lax.rem(130 - 4 * gx, 128), 128)
    spread = jnp.where(iota((32, 1024), 1) // 32 == iota((32, 1024), 0), 1.0, 0.0)
    wx[...] = dot(tx.T[0:16, 0:32], spread)


def odd_place(axis):
    return lax.rem(lax.axis_index(axis), 2) == 1


def choose(is_odd, low, high):
    return jnp.where(is_odd, low, high), jnp.where(is_odd, high, low)


def level2_rows(cells):
    return [
        sum(w * cells[2 * j + d] for d, w in weight.items() if 0 <= 2 * j + d < 16) for j in range(-1, 10)
    ]


def y_send(own, out_even, out_odd):
    row, column = iota((16, 32), 0), iota((16, 32), 1)
    y_matrix = fill(column - 2 * jnp.where(row < 8, row + 3, row - 1), weight).astype(bf16)
    row, column = iota((128, 128), 0), iota((128, 128), 1)
    z_matrix = jnp.where(column < 67, fill(row - 2 * jnp.where(column < 66, column, -1), weight), 0.0).astype(bf16)
    cells = own[...].astype(f32)
    wide = from_left(y_matrix, lanes(level2_rows(cells)), 3)
    tall = jnp.concatenate([wide[:, 128 * j : 128 * j + 128] for j in range(11)], axis=0)
    tall = from_right(tall, z_matrix, 3)
    lane = iota((8, 128), 1)

    def message(raw_at, share_at):
        rows, more = [cells[i, raw_at : raw_at + 8] for i in range(16)], jnp.zeros((8, 128), f32)
        for j in range(11):
            part = tall[16 * j + share_at : 16 * j + share_at + 8]
            first = part.astype(bf16).astype(f32)
            second = part - first
            rows.append(jnp.where(lane < 64, first, pltpu.roll(second, 64, 1)))
            beyond = jnp.where(lane % 8 < 4, pltpu.roll(first, (64 + 8 * j) % 128, 1), pltpu.roll(second, (68 + 8 * j) % 128, 1))
            more = jnp.where(lane // 8 == j, beyond, more)
        return jnp.concatenate([*rows, more], axis=0)

    even, odd = choose(odd_place("gy"), message(0, 0), message(24, 8))
    out_even[...] = even.astype(bf16)
    out_odd[...] = odd.astype(bf16)


def own_step(own, z_matrix, out):
    rows = level2_rows(own[...].astype(f32))
    out[...] = from_right(jnp.concatenate(rows, axis=0), z_matrix, 3).reshape(11, 32, 128)


def pack(parts, width, shift):
    slot = iota(parts[0].shape, 1) // width
    out = jnp.zeros(parts[0].shape, f32)
    for s, part in enumerate(parts):
        by = (width * s + shift) % 128
        moved = part if by == 0 else pltpu.roll(part, by, 1)
        out = jnp.where(slot == s, moved, out)
    return out


def y_step(own, from_odd, from_even, own_share, my1, my2, z_matrix, z_next, n1, n2, q3, out_even, out_odd):
    low, high = arrived("gy", from_even, from_odd, pl.ds(0, 224))
    low, high = low.astype(f32), high.astype(f32)
    cells = own[...].astype(f32)
    raw = [[part[8 * i : 8 * i + 8] for i in range(16)] for part in (low, high)]
    columns = lanes([jnp.concatenate([cells[i], raw[0][i], raw[1][i]], axis=0) for i in range(16)])
    terms = jnp.dot(my1[...], columns.astype(bf16), preferred_element_type=f32)
    done = terms[0:32] + terms[32:64]
    parts1 = [done[:, 128 * i : 128 * i + 128] for i in range(16)]

    sides = [level2_rows(part) for part in raw]
    tall = jnp.concatenate([part for j in range(11) for part in (sides[0][j], sides[1][j])], axis=0)
    tall = from_right(tall, z_matrix, 3)
    lane = iota((8, 128), 1)
    columns = []
    for j in range(11):
        stack = [own_share[j], tall[16 * j : 16 * j + 16]]
        for part in (low, high):
            body = part[128 + 8 * j : 136 + 8 * j]
            more = part[216:224] if j == 0 else pltpu.roll(part[216:224], 128 - 8 * j, 1)
            more = pltpu.roll(more + pltpu.roll(more, 124, 1), 64, 1)
            stack.append(jnp.where(lane < 64, body + pltpu.roll(body, 64, 1), jnp.where(lane < 67, more, 0.0)))
        columns.append(jnp.concatenate(stack, axis=0))
    wide = lanes(columns)
    data = split(wide, 3)
    first = my2[...].astype(bf16)
    rest = (my2[...] - first.astype(f32)).astype(bf16)
    both = jnp.dot(
        jnp.concatenate([first.astype(f32), rest.astype(f32)], axis=0).astype(bf16), data[0], preferred_element_type=f32
    )
    done = both[0:32] + both[32:64]
    for term in data[1:]:
        done = done + jnp.dot(first, term, preferred_element_type=f32)
    parts2 = [done[0:24, 128 * j : 128 * j + 128] for j in range(11)]
    half = {j - 1: done[24:32, 128 * j : 128 * j + 128] for j in range(11)}
    rows = [sum(w * half[2 * j + d] for d, w in weight.items() if 2 * j + d in half) for j in range(-2, 7)]
    tall = from_right(jnp.concatenate(rows, axis=0), z_next, 3)
    parts3 = [tall[8 * j : 8 * j + 8] for j in range(9)]
    for i in range(16):
        n1[i] = parts1[i]
    for j in range(11):
        n2[j] = parts2[j]
    for j in range(9):
        q3[j] = parts3[j]

    lane = iota((24, 128), 1)
    edge = [jnp.where(lane < 10, part, pltpu.roll(part, 72, 1)) for part in parts2]
    to_low = [pack(parts1, 8, 0), pack(edge[0:8], 16, 0), pack(edge[8:11], 16, 0), pack(parts3, 8, -35)]
    to_high = [pack(parts1, 8, 8), pack(parts2[0:8], 16, -55), pack(parts2[8:11], 16, -55), pack(parts3, 8, -32)]
    out_even[...], out_odd[...] = choose(
        odd_place("gz"), jnp.concatenate(to_low, axis=0), jnp.concatenate(to_high, axis=0)
    )


def arrived(axis, from_even, from_odd, rows):
    is_odd = odd_place(axis)
    even_part, odd_part = from_even[rows, :], from_odd[rows, :]
    return jnp.where(is_odd, even_part, odd_part), jnp.where(is_odd, odd_part, even_part)


def windows(low, high, slot, width):
    down = (128 - width * slot) % 128
    up = (128 + width - width * slot) % 128
    low = low if down == 0 else pltpu.roll(low, down, 1)
    high = high if up == 0 else pltpu.roll(high, up, 1)
    return jnp.where(iota(low.shape, 1) < width, low, high)


def q3_z_step(q3, from_odd, from_even, out, to_low, to_high):
    low, high = arrived("gz", from_even, from_odd, pl.ds(80, 8))
    lane = iota((8, 128), 1)
    rows = []
    for j in range(9):
        below = low if j == 0 else pltpu.roll(low, 128 - 8 * j, 1)
        above = pltpu.roll(high, (158 - 8 * j) % 128, 1)
        edge = jnp.where(lane < 3, below, jnp.where(lane >= 30, above, 0.0))
        rows.append(jnp.where(lane < 32, q3[j] + edge, 0.0))
    out[...] = pack(rows[2:6], 32, 0)
    to_low[...] = pack([jnp.zeros((8, 128), f32)] * 2 + rows[0:2], 32, 0)
    to_high[...] = pack(rows[6:9], 32, 0)


def q3_x_step(low, own, high, out):
    block = own[...] + low[...] + high[...]
    pair = jnp.concatenate([block, block], axis=0).astype(bf16)
    out[...] = jnp.broadcast_to(pair[None], (32, 16, 128))


def near_z_step(n1, n2, from_odd, from_even, mz1, mz2, n1_out, n2_out, to_low, to_high, to_even, to_odd):
    low, high = arrived("gz", from_even, from_odd, pl.ds(0, 32))
    rows = jnp.concatenate([lanes([n1[i], windows(low, high, i, 8)]) for i in range(16)], axis=0)
    done1 = dot(rows, mz1[...])
    n1_out[...] = done1.reshape(16, 32, 128)
    rows = []
    for g in range(2):
        low, high = arrived("gz", from_even, from_odd, pl.ds(32 + 24 * g, 24))
        rows += [lanes([n2[j], windows(low, high, j % 8, 16)]) for j in range(8 * g, min(8 * g + 8, 11))]
    done2 = dot(jnp.concatenate(rows, axis=0), mz2[...])
    n2_out[...] = done2.reshape(11, 24, 128)
    to_low[0:256] = done1[0:256]
    to_high[0:256] = done1[256:512]
    to_low[256:520] = done2
    to_high[256:520] = done2
    odd_chip = lax.rem(lax.axis_index("gx") // 2, 2) == 1
    to_even[...], to_odd[...] = choose(odd_chip, done2[0:72], done2[192:264])


def near_x_step(taps, n1, n2, even2, odd2, high, low, n1_out, n2_out):
    odd_chip = lax.rem(lax.axis_index("gx") // 2, 2) == 1
    low2 = jnp.where(odd_chip, even2[...], odd2[...])
    high2 = jnp.where(odd_chip, odd2[...], even2[...])
    for t in range(4):
        f = {}
        for i in range(8):
            f[i - 8] = low[32 * i + 8 * t : 32 * i + 8 * t + 8]
            f[i + 16] = high[32 * i + 8 * t : 32 * i + 8 * t + 8]
        for i in range(16):
            f[i] = n1[i, 8 * t : 8 * t + 8]
        for i in range(16):
            total = taps[0, 0] * f[i - 8]
            for a in range(-7, 9):
                total = total + taps[0, a + 8] * f[i + a]
            n1_out[i, 8 * t : 8 * t + 8] = total
    for t in range(3):
        half = {}
        for j in range(-1, 10):
            at = 256 + 24 * (j + 1) + 8 * t
            for place, part in ((j - 8, low[at : at + 8]), (j, n2[j + 1, 8 * t : 8 * t + 8]), (j + 8, high[at : at + 8])):
                half[place] = half[place] + part if place in half else part
        for k in range(3):
            at = 24 * k + 8 * t
            half[k - 9] = half[k - 9] + low2[at : at + 8]
            half[k + 15] = half[k + 15] + high2[at : at + 8]
        for i in range(-1, 10):
            total = taps[1, 0] * half[i - 8]
            for a in range(-7, 9):
                total = total + taps[1, a + 8] * half[i + a]
            n2_out[i + 1, 8 * t : 8 * t + 8] = total


def top_step(gathered, wz1, wz2, my, out):
    whole = gathered[...].astype(f32).reshape(8, 8, 8, 128)
    rows = lanes([whole[:, g].reshape(64, 128) for g in range(8)]).astype(bf16)
    along_z = jnp.dot(rows, wz1[...], preferred_element_type=f32)
    along_z = along_z + jnp.dot(rows, wz2[...], preferred_element_type=f32)
    done = dot(my[...], along_z)
    row = iota((16, 128), 0)
    block, past = done[:, 0:128], jnp.where(iota((16, 128), 1) % 32 // 5 == row % 5, done[:, 128:256], 0.0)
    for t in range(3):
        mine = (row // 5 == t) & (row < 13)
        block = jnp.where(row == 13 + t, jnp.sum(jnp.where(mine, past, 0.0), axis=0, keepdims=True), block)
    out[...] = jnp.broadcast_to(block[None], (8, 16, 128))


def raise_rows(rows, first, last):
    out = {}
    for i in range(first, last + 1):
        if i % 2 == 0:
            out[i] = rows[i // 2]
        else:
            j = (i - 1) // 2
            out[i] = (9.0 / 16.0) * (rows[j] + rows[j + 1]) - (1.0 / 16.0) * (rows[j - 1] + rows[j + 2])
    return out


def last_step(top, wx, n1, n2, y1, z1, y2, z2, out):
    e3 = {}
    row, lane = iota((16, 128), 0), iota((16, 128), 1)
    here = (lane >= 32) & (lane < 57) & (lane % 32 // 5 == row % 5)
    for i in range(9):
        total = None
        for g in range(8):
            term = wx[i : i + 1, 128 * g : 128 * g + 128] * top[g]
            total = term if total is None else total + term
        total = total + pltpu.roll(total, 64, 1)
        total = total + pltpu.roll(total, 32, 1)
        past = jnp.where(row < 5, total[13:14], jnp.where(row < 10, total[14:15], total[15:16]))
        e3[i - 2] = jnp.where(lane < 32, total, jnp.where(here, past, 0.0))
    e2 = raise_rows(e3, -1, 9)
    wide = from_left(y1, lanes([e2[i] for i in range(-1, 10)]))
    tall = jnp.concatenate([wide[:, 128 * i : 128 * i + 128] for i in range(11)], axis=0)
    tall = from_right(tall, z1) + n2[...].reshape(264, 128)
    tall = from_right(tall, z2)
    wide = from_left(y2, lanes([tall[24 * i : 24 * i + 24] for i in range(11)]))
    rows = raise_rows({i - 1: wide[:, 128 * i : 128 * i + 128] for i in range(11)}, 0, 15)
    for i in range(16):
        out[i] = rows[i] + n1[i]


def per_device(charge, kernel_taps, top_x, top_y, top_z):
    def shift(block, by):
        return lax.ppermute(block, "gx", [(i, (i + by) % 8) for i in range(8)])

    z_matrix = jnp.asarray(z_first, bf16)
    to_even, to_odd = call(y_send, [((224, 128), bf16)] * 2, [charge])
    from_odd = lax.ppermute(to_odd, "gy", swap_odd)
    from_even = lax.ppermute(to_even, "gy", swap_even)
    my1, my2 = call(
        prep_y, [((64, 48), bf16), ((32, 64), f32)], [kernel_taps, jnp.asarray(y_sources)], smem=(0,)
    )
    mz1, mz2 = call(prep_z, [((256, 128), f32)] * 2, [kernel_taps], smem=(0,))
    (own_share,) = call(own_step, [((11, 32, 128), f32)], [charge, z_matrix], after=[to_odd])
    wz1, wz2, ty, wx = call(
        prep_top,
        [((1024, 256), bf16)] * 2 + [((16, 64), f32), ((16, 1024), f32)],
        [top_x[None], top_y[None], top_z[None]],
    )

    n1, n2, q3, to_even, to_odd = call(
        y_step,
        [((16, 32, 128), f32), ((11, 24, 128), f32), ((9, 8, 128), f32), ((88, 128), f32), ((88, 128), f32)],
        [charge, from_odd, from_even, own_share, my1, my2, z_matrix, jnp.asarray(z_second, bf16)],
        after=[mz1, wx],
    )
    from_odd = lax.ppermute(to_odd, "gz", swap_odd)
    from_even = lax.ppermute(to_even, "gz", swap_even)

    q3, to_low, to_high = call(q3_z_step, [((8, 128), f32)] * 3, [q3, from_odd, from_even])
    (message,) = call(q3_x_step, [((32, 16, 128), bf16)], [shift(to_low, -1), q3, shift(to_high, 1)])
    gathered = lax.all_to_all(
        message.reshape(64, 8, 128), ("gy", "gz"), split_axis=0, concat_axis=0, tiled=True
    )
    n1, n2, to_low, to_high, to_even, to_odd = call(
        near_z_step,
        [((16, 32, 128), f32), ((11, 24, 128), f32)] + [((520, 128), f32)] * 2 + [((72, 128), f32)] * 2,
        [n1, n2, from_odd, from_even, mz1, mz2], after=[message],
    )
    halos = [
        lax.ppermute(to_even, "gx", [(0, 2), (2, 0), (1, 3), (3, 1), (4, 6), (6, 4), (5, 7), (7, 5)]),
        lax.ppermute(to_odd, "gx", [(2, 4), (4, 2), (3, 5), (5, 3), (6, 0), (0, 6), (7, 1), (1, 7)]),
        shift(to_low, -1),
        shift(to_high, 1),
    ]
    n1, n2 = call(
        near_x_step, [((16, 32, 128), f32), ((11, 24, 128), f32)],
        [kernel_taps, n1, n2, *halos], smem=(0,),
    )
    (message,) = call(top_step, [((8, 16, 128), f32)], [gathered, wz1, wz2, ty], after=[n1])
    top = lax.all_to_all(message, "gx", split_axis=0, concat_axis=0, tiled=True)
    (result,) = call(
        last_step, [((16, 32, 128), f32)],
        [top, wx, n1, n2, *(jnp.asarray(m, bf16) for m in (y_raise_top, z_raise_top, y_raise, z_raise))],
    )
    return result


def solution(mesh):
    return jax.shard_map(
        per_device,
        mesh=mesh,
        in_specs=(P("gx", "gy", "gz"), P(), P(), P(), P()),
        out_specs=P("gx", "gy", "gz"),
        check_vma=False,
    )
```

```python
import jax
import jax.numpy as jnp
import numpy as np
from jax import lax
from jax.experimental import pallas as pl
from jax.experimental.pallas import tpu as pltpu
from jax.sharding import PartitionSpec as P

f32 = jnp.float32
bf16 = jnp.bfloat16
highest = lax.Precision.HIGHEST
weight = {-3: -1.0 / 16.0, -1: 9.0 / 16.0, 0: 1.0, 1: 9.0 / 16.0, 3: -1.0 / 16.0}

twice = {}
for d0, w0 in weight.items():
    for d1, w1 in weight.items():
        twice[d0 + 2 * d1] = twice.get(d0 + 2 * d1, 0.0) + w0 * w1

swap_even = [(0, 1), (1, 0), (2, 3), (3, 2), (4, 5), (5, 4), (6, 7), (7, 6)]
swap_odd = [(1, 2), (2, 1), (3, 4), (4, 3), (5, 6), (6, 5), (7, 0), (0, 7)]


def table(rows, cols, entry):
    return np.array([[entry(r, c) for c in range(cols)] for r in range(rows)], np.float32)


def restrict(cell, coarse):
    return weight.get(cell - 2 * coarse, 0.0)


z_level2 = [*range(66), -1]
z_top = [*range(35), -2, -1]
z_first = table(128, 128, lambda r, c: restrict(r, z_level2[c]) if c < 67 else 0.0)
z_second = table(128, 128, lambda r, c: restrict(z_level2[r], z_top[c]) if r < 67 and c < 37 else 0.0)


def y_source(row, col):
    coarse = row - 9
    if row >= 35:
        return 0.0
    if col < 32:
        return restrict(col, coarse)
    if col < 40:
        return restrict(col - 40, coarse) if -2 <= coarse <= 1 else 0.0
    if col < 48:
        return restrict(col - 8, coarse) if 15 <= coarse <= 18 else 0.0
    if col < 56:
        return 1.0 if coarse == col - 57 and col < 55 else 0.0
    return 1.0 if coarse == col - 37 and col < 63 else 0.0


y_sources = table(40, 64, y_source)
y_raise_top = table(24, 16, lambda r, c: weight.get((r - 1) - 2 * (c - 2), 0.0) if r < 19 and c < 13 else 0.0)
z_raise_top = table(
    128,
    128,
    lambda r, c: weight.get((c - 1) - 2 * ((r if r < 32 else 32 + (r - 32) % 5) - 2), 0.0) if r < 57 and c < 67 else 0.0,
)
y_raise = table(32, 24, lambda r, c: weight.get(r - 2 * (c - 1), 0.0) if c < 19 else 0.0)
z_raise = table(128, 128, lambda r, c: weight.get(c - 2 * (r - 1), 0.0) if r < 67 else 0.0)

y_raise_both = y_raise @ y_raise_top
z_raise_both = z_raise_top @ z_raise


def dot(a, b):
    return jnp.dot(a, b, precision=highest, preferred_element_type=f32)


def split(x, count):
    terms = []
    for _ in range(count):
        terms.append(x.astype(bf16))
        x = x - terms[-1].astype(f32)
    return terms


def from_left(m, x, count=2):
    return sum(jnp.dot(m[...], term, preferred_element_type=f32) for term in split(x, count))


def from_right(x, m, count=2):
    return sum(jnp.dot(term, m[...], preferred_element_type=f32) for term in split(x, count))


def lanes(parts):
    return jnp.concatenate(parts, axis=1)


def iota(shape, dim):
    return lax.broadcasted_iota(jnp.int32, shape, dim)


def call(body, outs, args, smem=(), after=(), flops=1_000_000, bytes_accessed=1_000_000):

    def kernel(*refs):
        body(*refs[: len(args)], *refs[len(args) + len(after) :])

    return pl.pallas_call(
        kernel,
        out_shape=[jax.ShapeDtypeStruct(s, d) for s, d in outs],
        in_specs=[
            pl.BlockSpec(memory_space=pltpu.SMEM if i in smem else pltpu.VMEM)
            for i in range(len(args))
        ]
        + [pl.BlockSpec(memory_space=pl.ANY) for _ in after],
        out_specs=[pl.BlockSpec(memory_space=pltpu.VMEM) for _ in outs],
        compiler_params=pltpu.CompilerParams(vmem_limit_bytes=32 * 1024 * 1024),
        cost_estimate=pl.CostEstimate(
            flops=flops, bytes_accessed=bytes_accessed, transcendentals=0
        ),
        name=body.__name__,
    )(*args, *after)


def fill(gap, values):
    out = jnp.zeros(gap.shape, f32)
    for m, value in values.items():
        out = jnp.where(gap == m, value, out)
    return out


def prep_y(taps, sources, my1, my2):
    column = iota((32, 48), 1)
    cell = jnp.where(column < 32, column, jnp.where(column < 40, column - 40, column - 8))
    terms = split(fill(cell - iota((32, 48), 0), {m: taps[0, m + 8] for m in range(-8, 9)}), 2)
    my1[...] = jnp.concatenate([term.astype(f32) for term in terms], axis=0).astype(bf16)
    coarse = iota((24, 40), 1) - 9
    near = fill(coarse - (iota((24, 40), 0) - 1), {m: taps[1, m + 8] for m in range(-8, 9)})
    top = fill(iota((8, 40), 1) - 9 - 2 * iota((8, 40), 0), weight)
    my2[...] = dot(jnp.concatenate([near, top], axis=0), sources[...])


def prep_z(taps, mz1, mz2):
    far_off = 1 << 20
    row = iota((256, 128), 0)
    cell = jnp.where(row < 128, row, jnp.where(row < 136, row - 136, row - 8))
    cell = jnp.where(row < 144, cell, far_off)
    mz1[...] = fill(cell - iota((256, 128), 1), {m: taps[0, m + 8] for m in range(-8, 9)})
    own = jnp.where(row < 66, row, jnp.where(row == 66, -1, far_off))
    below = jnp.where(row < 139, row - 137, far_off)
    above = jnp.where(row < 154, row - 80, jnp.where(row == 154, 63, far_off))
    cell = jnp.where(row < 128, own, jnp.where(row < 144, below, above))
    mz2[...] = fill(cell - (iota((256, 128), 1) - 1), {m: taps[1, m + 8] for m in range(-8, 9)})


def toeplitz(profile, shift, size):
    start = pltpu.roll(jnp.broadcast_to(profile, (8, size)), shift, 1)[0:1]
    return pltpu.roll(jnp.broadcast_to(start, (size, size)), 0, 1, stride=1, stride_axis=0)


def prep_top(top_x, top_y, top_z, wz1, wz2, my, wx):
    gx, gy, gz = lax.axis_index("gx"), lax.axis_index("gy"), lax.axis_index("gz")
    tz = toeplitz(top_z[...], lax.rem(258 - 32 * gz, 256), 256)
    lane = iota((256, 128), 1)
    near, past = tz[:, 0:128], jnp.zeros((256, 128), f32)
    for t in range(5):
        past = jnp.where(lane // 5 == t, pltpu.roll(near, 96 + 5 * t, 1), past)
    near, past = jnp.where(lane < 32, near, 0.0), jnp.where(lane < 25, past, 0.0)
    for a in range(4):
        both = lanes([pltpu.roll(part, 32 * a, 1) if a else part for part in (near, past)])
        for g in range(8):
            rows = pl.ds(128 * g + 32 * a, 32)
            wz1[rows, :], wz2[rows, :] = split(both[32 * g : 32 * g + 32], 2)
    ty = toeplitz(lanes([top_y[...]] * 2), lax.rem(130 - 8 * gy, 128), 128)
    my[...] = ty.T[0:16, 0:64]
    tx = toeplitz(lanes([top_x[...]] * 4), lax.rem(130 - 4 * gx, 128), 128)
    spread = jnp.where(iota((32, 1024), 1) // 32 == iota((32, 1024), 0), 1.0, 0.0)
    wx[...] = dot(tx.T[0:16, 0:32], spread)


def odd_place(axis):
    return lax.rem(lax.axis_index(axis), 2) == 1


def choose(is_odd, low, high):
    return jnp.where(is_odd, low, high), jnp.where(is_odd, high, low)


def level2_rows(cells):
    return [
        sum(w * cells[2 * j + d] for d, w in weight.items() if 0 <= 2 * j + d < 16) for j in range(-1, 10)
    ]


def y_send(own, out_even, out_odd):
    row, column = iota((16, 32), 0), iota((16, 32), 1)
    y_matrix = fill(column - 2 * jnp.where(row < 8, row + 3, row - 1), weight).astype(bf16)
    row, column = iota((128, 128), 0), iota((128, 128), 1)
    z_matrix = jnp.where(column < 67, fill(row - 2 * jnp.where(column < 66, column, -1), weight), 0.0).astype(bf16)
    cells = own[...].astype(f32)
    wide = from_left(y_matrix, lanes(level2_rows(cells)), 3)
    tall = jnp.concatenate([wide[:, 128 * j : 128 * j + 128] for j in range(11)], axis=0)
    tall = from_right(tall, z_matrix, 3)
    lane = iota((8, 128), 1)

    def message(raw_at, share_at):
        rows, more = [cells[i, raw_at : raw_at + 8] for i in range(16)], jnp.zeros((8, 128), f32)
        for j in range(11):
            part = tall[16 * j + share_at : 16 * j + share_at + 8]
            first = part.astype(bf16).astype(f32)
            second = part - first
            rows.append(jnp.where(lane < 64, first, pltpu.roll(second, 64, 1)))
            beyond = jnp.where(lane % 8 < 4, pltpu.roll(first, (64 + 8 * j) % 128, 1), pltpu.roll(second, (68 + 8 * j) % 128, 1))
            more = jnp.where(lane // 8 == j, beyond, more)
        return jnp.concatenate([*rows, more], axis=0)

    even, odd = choose(odd_place("gy"), message(0, 0), message(24, 8))
    out_even[...] = even.astype(bf16)
    out_odd[...] = odd.astype(bf16)


def own_step(own, z_matrix, out):
    rows = level2_rows(own[...].astype(f32))
    out[...] = from_right(jnp.concatenate(rows, axis=0), z_matrix, 3).reshape(11, 32, 128)


def pack(parts, width, shift):
    slot = iota(parts[0].shape, 1) // width
    out = jnp.zeros(parts[0].shape, f32)
    for s, part in enumerate(parts):
        by = (width * s + shift) % 128
        moved = part if by == 0 else pltpu.roll(part, by, 1)
        out = jnp.where(slot == s, moved, out)
    return out


def y_step(own, from_odd, from_even, own_share, my1, my2, z_matrix, z_next, n1, n2, q3, out_even, out_odd):
    low, high = arrived("gy", from_even, from_odd, pl.ds(0, 224))
    low, high = low.astype(f32), high.astype(f32)
    cells = own[...].astype(f32)
    raw = [[part[8 * i : 8 * i + 8] for i in range(16)] for part in (low, high)]
    columns = lanes([jnp.concatenate([cells[i], raw[0][i], raw[1][i]], axis=0) for i in range(16)])
    terms = jnp.dot(my1[...], columns.astype(bf16), preferred_element_type=f32)
    done = terms[0:32] + terms[32:64]
    parts1 = [done[:, 128 * i : 128 * i + 128] for i in range(16)]

    sides = [level2_rows(part) for part in raw]
    tall = jnp.concatenate([part for j in range(11) for part in (sides[0][j], sides[1][j])], axis=0)
    tall = from_right(tall, z_matrix, 3)
    lane = iota((8, 128), 1)
    columns = []
    for j in range(11):
        stack = [own_share[j], tall[16 * j : 16 * j + 16]]
        for part in (low, high):
            body = part[128 + 8 * j : 136 + 8 * j]
            more = part[216:224] if j == 0 else pltpu.roll(part[216:224], 128 - 8 * j, 1)
            more = pltpu.roll(more + pltpu.roll(more, 124, 1), 64, 1)
            stack.append(jnp.where(lane < 64, body + pltpu.roll(body, 64, 1), jnp.where(lane < 67, more, 0.0)))
        columns.append(jnp.concatenate(stack, axis=0))
    wide = lanes(columns)
    data = split(wide, 3)
    first = my2[...].astype(bf16)
    rest = (my2[...] - first.astype(f32)).astype(bf16)
    both = jnp.dot(
        jnp.concatenate([first.astype(f32), rest.astype(f32)], axis=0).astype(bf16), data[0], preferred_element_type=f32
    )
    done = both[0:32] + both[32:64]
    for term in data[1:]:
        done = done + jnp.dot(first, term, preferred_element_type=f32)
    parts2 = [done[0:24, 128 * j : 128 * j + 128] for j in range(11)]
    half = {j - 1: done[24:32, 128 * j : 128 * j + 128] for j in range(11)}
    rows = [sum(w * half[2 * j + d] for d, w in weight.items() if 2 * j + d in half) for j in range(-2, 7)]
    tall = from_right(jnp.concatenate(rows, axis=0), z_next, 3)
    parts3 = [tall[8 * j : 8 * j + 8] for j in range(9)]
    for i in range(16):
        n1[i] = parts1[i]
    for j in range(11):
        n2[j] = parts2[j]
    for j in range(9):
        q3[j] = parts3[j]

    lane = iota((24, 128), 1)
    edge = [jnp.where(lane < 10, part, pltpu.roll(part, 72, 1)) for part in parts2]
    to_low = [pack(parts1, 8, 0), pack(edge[0:8], 16, 0), pack(edge[8:11], 16, 0), pack(parts3, 8, -35)]
    to_high = [pack(parts1, 8, 8), pack(parts2[0:8], 16, -55), pack(parts2[8:11], 16, -55), pack(parts3, 8, -32)]
    out_even[...], out_odd[...] = choose(
        odd_place("gz"), jnp.concatenate(to_low, axis=0), jnp.concatenate(to_high, axis=0)
    )


def arrived(axis, from_even, from_odd, rows):
    is_odd = odd_place(axis)
    even_part, odd_part = from_even[rows, :], from_odd[rows, :]
    return jnp.where(is_odd, even_part, odd_part), jnp.where(is_odd, odd_part, even_part)


def windows(low, high, slot, width):
    down = (128 - width * slot) % 128
    up = (128 + width - width * slot) % 128
    low = low if down == 0 else pltpu.roll(low, down, 1)
    high = high if up == 0 else pltpu.roll(high, up, 1)
    return jnp.where(iota(low.shape, 1) < width, low, high)


def q3_z_step(q3, from_odd, from_even, out, to_low, to_high):
    low, high = arrived("gz", from_even, from_odd, pl.ds(80, 8))
    lane = iota((8, 128), 1)
    rows = []
    for j in range(9):
        below = low if j == 0 else pltpu.roll(low, 128 - 8 * j, 1)
        above = pltpu.roll(high, (158 - 8 * j) % 128, 1)
        edge = jnp.where(lane < 3, below, jnp.where(lane >= 30, above, 0.0))
        rows.append(jnp.where(lane < 32, q3[j] + edge, 0.0))
    out[...] = pack(rows[2:6], 32, 0)
    to_low[...] = pack([jnp.zeros((8, 128), f32)] * 2 + rows[0:2], 32, 0)
    to_high[...] = pack(rows[6:9], 32, 0)


def q3_x_step(low, own, high, out):
    block = own[...] + low[...] + high[...]
    pair = jnp.concatenate([block, block], axis=0).astype(bf16)
    out[...] = jnp.broadcast_to(pair[None], (32, 16, 128))


def near_z_step(n1, n2, from_odd, from_even, mz1, mz2, n1_out, n2_out, to_low, to_high, to_even, to_odd):
    low, high = arrived("gz", from_even, from_odd, pl.ds(0, 32))
    rows = jnp.concatenate([lanes([n1[i], windows(low, high, i, 8)]) for i in range(16)], axis=0)
    done1 = dot(rows, mz1[...])
    n1_out[...] = done1.reshape(16, 32, 128)
    rows = []
    for g in range(2):
        low, high = arrived("gz", from_even, from_odd, pl.ds(32 + 24 * g, 24))
        rows += [lanes([n2[j], windows(low, high, j % 8, 16)]) for j in range(8 * g, min(8 * g + 8, 11))]
    done2 = dot(jnp.concatenate(rows, axis=0), mz2[...])
    n2_out[...] = done2.reshape(11, 24, 128)
    to_low[0:256] = done1[0:256]
    to_high[0:256] = done1[256:512]
    to_low[256:520] = done2
    to_high[256:520] = done2
    odd_chip = lax.rem(lax.axis_index("gx") // 2, 2) == 1
    to_even[...], to_odd[...] = choose(odd_chip, done2[0:72], done2[192:264])


def near_x_step(taps, n1, n2, even2, odd2, high, low, y2, z2, out):
    odd_chip = lax.rem(lax.axis_index("gx") // 2, 2) == 1
    low2 = jnp.where(odd_chip, even2[...], odd2[...])
    high2 = jnp.where(odd_chip, odd2[...], even2[...])
    for t in range(4):
        f = {}
        for i in range(8):
            f[i - 8] = low[32 * i + 8 * t : 32 * i + 8 * t + 8]
            f[i + 16] = high[32 * i + 8 * t : 32 * i + 8 * t + 8]
        for i in range(16):
            f[i] = n1[i, 8 * t : 8 * t + 8]
        for i in range(16):
            total = taps[0, 0] * f[i - 8]
            for a in range(-7, 9):
                total = total + taps[0, a + 8] * f[i + a]
            out[i, 8 * t : 8 * t + 8] = total
    tiles = {}
    for t in range(3):
        half = {}
        for j in range(-1, 10):
            at = 256 + 24 * (j + 1) + 8 * t
            for place, part in ((j - 8, low[at : at + 8]), (j, n2[j + 1, 8 * t : 8 * t + 8]), (j + 8, high[at : at + 8])):
                half[place] = half[place] + part if place in half else part
        for k in range(3):
            at = 24 * k + 8 * t
            half[k - 9] = half[k - 9] + low2[at : at + 8]
            half[k + 15] = half[k + 15] + high2[at : at + 8]
        for i in range(-1, 10):
            total = taps[1, 0] * half[i - 8]
            for a in range(-7, 9):
                total = total + taps[1, a + 8] * half[i + a]
            tiles[i, t] = total
    tall = jnp.concatenate([tiles[i, t] for i in range(-1, 10) for t in range(3)], axis=0)
    tall = from_right(tall, z2)
    wide = from_left(y2, lanes([tall[24 * i : 24 * i + 24] for i in range(11)]))
    rows = raise_rows({i - 1: wide[:, 128 * i : 128 * i + 128] for i in range(11)}, 0, 15)
    for i in range(16):
        out[i] = out[i] + rows[i]


def top_step(gathered, wz1, wz2, my, out):
    whole = gathered[...].astype(f32).reshape(8, 8, 8, 128)
    rows = lanes([whole[:, g].reshape(64, 128) for g in range(8)]).astype(bf16)
    along_z = jnp.dot(rows, wz1[...], preferred_element_type=f32)
    along_z = along_z + jnp.dot(rows, wz2[...], preferred_element_type=f32)
    done = dot(my[...], along_z)
    row = iota((16, 128), 0)
    block, past = done[:, 0:128], jnp.where(iota((16, 128), 1) % 32 // 5 == row % 5, done[:, 128:256], 0.0)
    for t in range(3):
        mine = (row // 5 == t) & (row < 13)
        block = jnp.where(row == 13 + t, jnp.sum(jnp.where(mine, past, 0.0), axis=0, keepdims=True), block)
    out[...] = jnp.broadcast_to(block[None], (8, 16, 128))


def raise_rows(rows, first, last):
    out = {}
    for i in range(first, last + 1):
        if i % 2 == 0:
            out[i] = rows[i // 2]
        else:
            j = (i - 1) // 2
            out[i] = (9.0 / 16.0) * (rows[j] + rows[j + 1]) - (1.0 / 16.0) * (rows[j - 1] + rows[j + 2])
    return out


def last_step(top, wx, near, y_both, z_both, out):
    e3 = {}
    row, lane = iota((16, 128), 0), iota((16, 128), 1)
    here = (lane >= 32) & (lane < 57) & (lane % 32 // 5 == row % 5)
    for i in range(9):
        total = None
        for g in range(8):
            term = wx[i : i + 1, 128 * g : 128 * g + 128] * top[g]
            total = term if total is None else total + term
        total = total + pltpu.roll(total, 64, 1)
        total = total + pltpu.roll(total, 32, 1)
        past = jnp.where(row < 5, total[13:14], jnp.where(row < 10, total[14:15], total[15:16]))
        e3[i - 2] = jnp.where(lane < 32, total, jnp.where(here, past, 0.0))
    tall = from_right(jnp.concatenate([e3[i] for i in range(-2, 7)], axis=0), z_both)
    wide = from_left(y_both, lanes([tall[16 * i : 16 * i + 16] for i in range(9)]))
    rows = raise_rows({i - 2: wide[:, 128 * i : 128 * i + 128] for i in range(9)}, -1, 9)
    rows = raise_rows(rows, 0, 15)
    for i in range(16):
        out[i] = rows[i] + near[i]


def per_device(charge, kernel_taps, top_x, top_y, top_z):
    def shift(block, by):
        return lax.ppermute(block, "gx", [(i, (i + by) % 8) for i in range(8)])

    z_matrix = jnp.asarray(z_first, bf16)
    to_even, to_odd = call(y_send, [((224, 128), bf16)] * 2, [charge])
    from_odd = lax.ppermute(to_odd, "gy", swap_odd)
    from_even = lax.ppermute(to_even, "gy", swap_even)
    my1, my2 = call(
        prep_y, [((64, 48), bf16), ((32, 64), f32)], [kernel_taps, jnp.asarray(y_sources)], smem=(0,)
    )
    mz1, mz2 = call(prep_z, [((256, 128), f32)] * 2, [kernel_taps], smem=(0,))
    (own_share,) = call(own_step, [((11, 32, 128), f32)], [charge, z_matrix], after=[to_odd])
    wz1, wz2, ty, wx = call(
        prep_top,
        [((1024, 256), bf16)] * 2 + [((16, 64), f32), ((16, 1024), f32)],
        [top_x[None], top_y[None], top_z[None]],
    )

    n1, n2, q3, to_even, to_odd = call(
        y_step,
        [((16, 32, 128), f32), ((11, 24, 128), f32), ((9, 8, 128), f32), ((88, 128), f32), ((88, 128), f32)],
        [charge, from_odd, from_even, own_share, my1, my2, z_matrix, jnp.asarray(z_second, bf16)],
        after=[mz1, wx],
    )
    from_odd = lax.ppermute(to_odd, "gz", swap_odd)
    from_even = lax.ppermute(to_even, "gz", swap_even)

    q3, to_low, to_high = call(q3_z_step, [((8, 128), f32)] * 3, [q3, from_odd, from_even])
    (message,) = call(q3_x_step, [((32, 16, 128), bf16)], [shift(to_low, -1), q3, shift(to_high, 1)])
    gathered = lax.all_to_all(
        message.reshape(64, 8, 128), ("gy", "gz"), split_axis=0, concat_axis=0, tiled=True
    )
    n1, n2, to_low, to_high, to_even, to_odd = call(
        near_z_step,
        [((16, 32, 128), f32), ((11, 24, 128), f32)] + [((520, 128), f32)] * 2 + [((72, 128), f32)] * 2,
        [n1, n2, from_odd, from_even, mz1, mz2], after=[message],
    )
    halos = [
        lax.ppermute(to_even, "gx", [(0, 2), (2, 0), (1, 3), (3, 1), (4, 6), (6, 4), (5, 7), (7, 5)]),
        lax.ppermute(to_odd, "gx", [(2, 4), (4, 2), (3, 5), (5, 3), (6, 0), (0, 6), (7, 1), (1, 7)]),
        shift(to_low, -1),
        shift(to_high, 1),
    ]
    (near,) = call(
        near_x_step, [((16, 32, 128), f32)],
        [kernel_taps, n1, n2, *halos, jnp.asarray(y_raise, bf16), jnp.asarray(z_raise, bf16)], smem=(0,),
    )
    (message,) = call(top_step, [((8, 16, 128), f32)], [gathered, wz1, wz2, ty], after=[near])
    top = lax.all_to_all(message, "gx", split_axis=0, concat_axis=0, tiled=True)
    (result,) = call(
        last_step, [((16, 32, 128), f32)],
        [top, wx, near, jnp.asarray(y_raise_both, bf16), jnp.asarray(z_raise_both, bf16)],
    )
    return result


def solution(mesh):
    return jax.shard_map(
        per_device,
        mesh=mesh,
        in_specs=(P("gx", "gy", "gz"), P(), P(), P(), P()),
        out_specs=P("gx", "gy", "gz"),
        check_vma=False,
    )
```

```python
import jax
import jax.numpy as jnp
import numpy as np
from jax import lax
from jax.experimental import pallas as pl
from jax.experimental.pallas import tpu as pltpu
from jax.sharding import PartitionSpec as P

f32 = jnp.float32
bf16 = jnp.bfloat16
highest = lax.Precision.HIGHEST
weight = {-3: -1.0 / 16.0, -1: 9.0 / 16.0, 0: 1.0, 1: 9.0 / 16.0, 3: -1.0 / 16.0}

twice = {}
for d0, w0 in weight.items():
    for d1, w1 in weight.items():
        twice[d0 + 2 * d1] = twice.get(d0 + 2 * d1, 0.0) + w0 * w1

swap_even = [(0, 1), (1, 0), (2, 3), (3, 2), (4, 5), (5, 4), (6, 7), (7, 6)]
swap_odd = [(1, 2), (2, 1), (3, 4), (4, 3), (5, 6), (6, 5), (7, 0), (0, 7)]


def table(rows, cols, entry):
    return np.array([[entry(r, c) for c in range(cols)] for r in range(rows)], np.float32)


def restrict(cell, coarse):
    return weight.get(cell - 2 * coarse, 0.0)


z_level2 = [*range(66), -1]
z_top = [*range(35), -2, -1]
z_first = table(128, 128, lambda r, c: restrict(r, z_level2[c]) if c < 67 else 0.0)
z_second = table(128, 128, lambda r, c: restrict(z_level2[r], z_top[c]) if r < 67 and c < 37 else 0.0)


def y_source(row, col):
    coarse = row - 9
    if row >= 35:
        return 0.0
    if col < 32:
        return restrict(col, coarse)
    if col < 40:
        return restrict(col - 40, coarse) if -2 <= coarse <= 1 else 0.0
    if col < 48:
        return restrict(col - 8, coarse) if 15 <= coarse <= 18 else 0.0
    if col < 56:
        return 1.0 if coarse == col - 57 and col < 55 else 0.0
    return 1.0 if coarse == col - 37 and col < 63 else 0.0


y_sources = table(40, 64, y_source)
y_raise_top = table(24, 16, lambda r, c: weight.get((r - 1) - 2 * (c - 2), 0.0) if r < 19 and c < 13 else 0.0)
z_raise_top = table(
    128,
    128,
    lambda r, c: weight.get((c - 1) - 2 * ((r if r < 32 else 32 + (r - 32) % 5) - 2), 0.0) if r < 57 and c < 67 else 0.0,
)
y_raise = table(32, 24, lambda r, c: weight.get(r - 2 * (c - 1), 0.0) if c < 19 else 0.0)
z_raise = table(128, 128, lambda r, c: weight.get(c - 2 * (r - 1), 0.0) if r < 67 else 0.0)

y_raise_both = y_raise @ y_raise_top
z_raise_both = z_raise_top @ z_raise


def dot(a, b):
    return jnp.dot(a, b, precision=highest, preferred_element_type=f32)


def split(x, count):
    terms = []
    for _ in range(count):
        terms.append(x.astype(bf16))
        x = x - terms[-1].astype(f32)
    return terms


def from_left(m, x, count=2):
    return sum(jnp.dot(m[...], term, preferred_element_type=f32) for term in split(x, count))


def from_right(x, m, count=2):
    return sum(jnp.dot(term, m[...], preferred_element_type=f32) for term in split(x, count))


def lanes(parts):
    return jnp.concatenate(parts, axis=1)


def iota(shape, dim):
    return lax.broadcasted_iota(jnp.int32, shape, dim)


def call(body, outs, args, smem=(), after=(), flops=1_000_000, bytes_accessed=1_000_000):

    def kernel(*refs):
        body(*refs[: len(args)], *refs[len(args) + len(after) :])

    return pl.pallas_call(
        kernel,
        out_shape=[jax.ShapeDtypeStruct(s, d) for s, d in outs],
        in_specs=[
            pl.BlockSpec(memory_space=pltpu.SMEM if i in smem else pltpu.VMEM)
            for i in range(len(args))
        ]
        + [pl.BlockSpec(memory_space=pl.ANY) for _ in after],
        out_specs=[pl.BlockSpec(memory_space=pltpu.VMEM) for _ in outs],
        compiler_params=pltpu.CompilerParams(vmem_limit_bytes=32 * 1024 * 1024),
        cost_estimate=pl.CostEstimate(
            flops=flops, bytes_accessed=bytes_accessed, transcendentals=0
        ),
        name=body.__name__,
    )(*args, *after)


def fill(gap, values):
    out = jnp.zeros(gap.shape, f32)
    for m, value in values.items():
        out = jnp.where(gap == m, value, out)
    return out


def prep_y(taps, sources, my1, my2):
    column = iota((32, 48), 1)
    cell = jnp.where(column < 32, column, jnp.where(column < 40, column - 40, column - 8))
    terms = split(fill(cell - iota((32, 48), 0), {m: taps[0, m + 8] for m in range(-8, 9)}), 2)
    my1[...] = jnp.concatenate([term.astype(f32) for term in terms], axis=0).astype(bf16)
    coarse = iota((24, 40), 1) - 9
    near = fill(coarse - (iota((24, 40), 0) - 1), {m: taps[1, m + 8] for m in range(-8, 9)})
    top = fill(iota((8, 40), 1) - 9 - 2 * iota((8, 40), 0), weight)
    my2[...] = dot(jnp.concatenate([near, top], axis=0), sources[...])


def prep_z(taps, mz1, mz2):
    far_off = 1 << 20
    row = iota((256, 128), 0)
    cell = jnp.where(row < 128, row, jnp.where(row < 136, row - 136, row - 8))
    cell = jnp.where(row < 144, cell, far_off)
    mz1[...] = fill(cell - iota((256, 128), 1), {m: taps[0, m + 8] for m in range(-8, 9)})
    own = jnp.where(row < 66, row, jnp.where(row == 66, -1, far_off))
    below = jnp.where(row < 139, row - 137, far_off)
    above = jnp.where(row < 154, row - 80, jnp.where(row == 154, 63, far_off))
    cell = jnp.where(row < 128, own, jnp.where(row < 144, below, above))
    mz2[...] = fill(cell - (iota((256, 128), 1) - 1), {m: taps[1, m + 8] for m in range(-8, 9)})


def toeplitz(profile, shift, size):
    start = pltpu.roll(jnp.broadcast_to(profile, (8, size)), shift, 1)[0:1]
    return pltpu.roll(jnp.broadcast_to(start, (size, size)), 0, 1, stride=1, stride_axis=0)


def prep_top(top_x, top_y, top_z, wz1, wz2, my, wx):
    gx, gy, gz = lax.axis_index("gx"), lax.axis_index("gy"), lax.axis_index("gz")
    tz = toeplitz(top_z[...], lax.rem(258 - 32 * gz, 256), 256)
    lane = iota((256, 128), 1)
    near, past = tz[:, 0:128], jnp.zeros((256, 128), f32)
    for t in range(5):
        past = jnp.where(lane // 5 == t, pltpu.roll(near, 96 + 5 * t, 1), past)
    near, past = jnp.where(lane < 32, near, 0.0), jnp.where(lane < 25, past, 0.0)
    for a in range(4):
        both = lanes([pltpu.roll(part, 32 * a, 1) if a else part for part in (near, past)])
        for g in range(8):
            rows = pl.ds(128 * g + 32 * a, 32)
            wz1[rows, :], wz2[rows, :] = split(both[32 * g : 32 * g + 32], 2)
    ty = toeplitz(lanes([top_y[...]] * 2), lax.rem(130 - 8 * gy, 128), 128)
    my[...] = ty.T[0:16, 0:64]
    tx = toeplitz(lanes([top_x[...]] * 4), lax.rem(130 - 4 * gx, 128), 128)
    spread = jnp.where(iota((32, 1024), 1) // 32 == iota((32, 1024), 0), 1.0, 0.0)
    wx[...] = dot(tx.T[0:16, 0:32], spread)


def odd_place(axis):
    return lax.rem(lax.axis_index(axis), 2) == 1


def choose(is_odd, low, high):
    return jnp.where(is_odd, low, high), jnp.where(is_odd, high, low)


def level2_rows(cells):
    return [
        sum(w * cells[2 * j + d] for d, w in weight.items() if 0 <= 2 * j + d < 16) for j in range(-1, 10)
    ]


def y_send(own, out_even, out_odd):
    row, column = iota((16, 32), 0), iota((16, 32), 1)
    y_matrix = fill(column - 2 * jnp.where(row < 8, row + 3, row - 1), weight).astype(bf16)
    row, column = iota((128, 128), 0), iota((128, 128), 1)
    z_matrix = jnp.where(column < 67, fill(row - 2 * jnp.where(column < 66, column, -1), weight), 0.0).astype(bf16)
    cells = own[...].astype(f32)
    wide = from_left(y_matrix, lanes(level2_rows(cells)), 3)
    tall = jnp.concatenate([wide[:, 128 * j : 128 * j + 128] for j in range(11)], axis=0)
    tall = from_right(tall, z_matrix, 3)
    lane = iota((8, 128), 1)

    def message(raw_at, share_at):
        rows, more = [cells[i, raw_at : raw_at + 8] for i in range(16)], jnp.zeros((8, 128), f32)
        for j in range(11):
            part = tall[16 * j + share_at : 16 * j + share_at + 8]
            first = part.astype(bf16).astype(f32)
            second = part - first
            rows.append(jnp.where(lane < 64, first, pltpu.roll(second, 64, 1)))
            beyond = jnp.where(lane % 8 < 4, pltpu.roll(first, (64 + 8 * j) % 128, 1), pltpu.roll(second, (68 + 8 * j) % 128, 1))
            more = jnp.where(lane // 8 == j, beyond, more)
        return jnp.concatenate([*rows, more], axis=0)

    even, odd = choose(odd_place("gy"), message(0, 0), message(24, 8))
    out_even[...] = even.astype(bf16)
    out_odd[...] = odd.astype(bf16)


def own_step(own, z_matrix, out):
    rows = level2_rows(own[...].astype(f32))
    out[...] = from_right(jnp.concatenate(rows, axis=0), z_matrix, 3).reshape(11, 32, 128)


def pack(parts, width, shift):
    slot = iota(parts[0].shape, 1) // width
    out = jnp.zeros(parts[0].shape, f32)
    for s, part in enumerate(parts):
        by = (width * s + shift) % 128
        moved = part if by == 0 else pltpu.roll(part, by, 1)
        out = jnp.where(slot == s, moved, out)
    return out


def y_step(own, from_odd, from_even, own_share, my1, my2, z_matrix, z_next, n1, n2, q3, out_even, out_odd):
    low, high = arrived("gy", from_even, from_odd, pl.ds(0, 224))
    low, high = low.astype(f32), high.astype(f32)
    cells = own[...].astype(f32)
    raw = [[part[8 * i : 8 * i + 8] for i in range(16)] for part in (low, high)]
    columns = lanes([jnp.concatenate([cells[i], raw[0][i], raw[1][i]], axis=0) for i in range(16)])
    terms = jnp.dot(my1[...], columns.astype(bf16), preferred_element_type=f32)
    done = terms[0:32] + terms[32:64]
    parts1 = [done[:, 128 * i : 128 * i + 128] for i in range(16)]

    sides = [level2_rows(part) for part in raw]
    tall = jnp.concatenate([part for j in range(11) for part in (sides[0][j], sides[1][j])], axis=0)
    tall = from_right(tall, z_matrix, 3)
    lane = iota((8, 128), 1)
    columns = []
    for j in range(11):
        stack = [own_share[j], tall[16 * j : 16 * j + 16]]
        for part in (low, high):
            body = part[128 + 8 * j : 136 + 8 * j]
            more = part[216:224] if j == 0 else pltpu.roll(part[216:224], 128 - 8 * j, 1)
            more = pltpu.roll(more + pltpu.roll(more, 124, 1), 64, 1)
            stack.append(jnp.where(lane < 64, body + pltpu.roll(body, 64, 1), jnp.where(lane < 67, more, 0.0)))
        columns.append(jnp.concatenate(stack, axis=0))
    wide = lanes(columns)
    data = split(wide, 3)
    first = my2[...].astype(bf16)
    rest = (my2[...] - first.astype(f32)).astype(bf16)
    both = jnp.dot(
        jnp.concatenate([first.astype(f32), rest.astype(f32)], axis=0).astype(bf16), data[0], preferred_element_type=f32
    )
    done = both[0:32] + both[32:64]
    for term in data[1:]:
        done = done + jnp.dot(first, term, preferred_element_type=f32)
    parts2 = [done[0:24, 128 * j : 128 * j + 128] for j in range(11)]
    half = {j - 1: done[24:32, 128 * j : 128 * j + 128] for j in range(11)}
    rows = [sum(w * half[2 * j + d] for d, w in weight.items() if 2 * j + d in half) for j in range(-2, 7)]
    tall = from_right(jnp.concatenate(rows, axis=0), z_next, 3)
    parts3 = [tall[8 * j : 8 * j + 8] for j in range(9)]
    for i in range(16):
        n1[i] = parts1[i]
    for j in range(11):
        n2[j] = parts2[j]
    for j in range(9):
        q3[j] = parts3[j]

    lane = iota((24, 128), 1)
    edge = [jnp.where(lane < 10, part, pltpu.roll(part, 72, 1)) for part in parts2]
    to_low = [pack(parts1, 8, 0), pack(edge[0:8], 16, 0), pack(edge[8:11], 16, 0), pack(parts3, 8, -35)]
    to_high = [pack(parts1, 8, 8), pack(parts2[0:8], 16, -55), pack(parts2[8:11], 16, -55), pack(parts3, 8, -32)]
    out_even[...], out_odd[...] = choose(
        odd_place("gz"), jnp.concatenate(to_low, axis=0), jnp.concatenate(to_high, axis=0)
    )


def arrived(axis, from_even, from_odd, rows):
    is_odd = odd_place(axis)
    even_part, odd_part = from_even[rows, :], from_odd[rows, :]
    return jnp.where(is_odd, even_part, odd_part), jnp.where(is_odd, odd_part, even_part)


def windows(low, high, slot, width):
    down = (128 - width * slot) % 128
    up = (128 + width - width * slot) % 128
    low = low if down == 0 else pltpu.roll(low, down, 1)
    high = high if up == 0 else pltpu.roll(high, up, 1)
    return jnp.where(iota(low.shape, 1) < width, low, high)


def q3_z_step(q3, from_odd, from_even, out, to_low, to_high):
    low, high = arrived("gz", from_even, from_odd, pl.ds(80, 8))
    lane = iota((8, 128), 1)
    rows = []
    for j in range(9):
        below = low if j == 0 else pltpu.roll(low, 128 - 8 * j, 1)
        above = pltpu.roll(high, (158 - 8 * j) % 128, 1)
        edge = jnp.where(lane < 3, below, jnp.where(lane >= 30, above, 0.0))
        rows.append(jnp.where(lane < 32, q3[j] + edge, 0.0))
    out[...] = pack(rows[2:6], 32, 0)
    to_low[...] = pack([jnp.zeros((8, 128), f32)] * 2 + rows[0:2], 32, 0)
    to_high[...] = pack(rows[6:9], 32, 0)


def q3_x_step(low, own, high, out):
    block = own[...] + low[...] + high[...]
    pair = jnp.concatenate([block, block], axis=0).astype(bf16)
    out[...] = jnp.broadcast_to(pair[None], (32, 16, 128))


def near_z_step(n1, n2, from_odd, from_even, mz1, mz2, n1_out, n2_out, to_low, to_high, to_even, to_odd):
    low, high = arrived("gz", from_even, from_odd, pl.ds(0, 32))
    rows = jnp.concatenate([lanes([n1[i], windows(low, high, i, 8)]) for i in range(16)], axis=0)
    done1 = dot(rows, mz1[...])
    n1_out[...] = done1.reshape(16, 32, 128)
    rows = []
    for g in range(2):
        low, high = arrived("gz", from_even, from_odd, pl.ds(32 + 24 * g, 24))
        rows += [lanes([n2[j], windows(low, high, j % 8, 16)]) for j in range(8 * g, min(8 * g + 8, 11))]
    done2 = dot(jnp.concatenate(rows, axis=0), mz2[...])
    n2_out[...] = done2.reshape(11, 24, 128)
    to_low[0:256] = done1[0:256]
    to_high[0:256] = done1[256:512]
    to_low[256:520] = done2
    to_high[256:520] = done2
    odd_chip = lax.rem(lax.axis_index("gx") // 2, 2) == 1
    to_even[...], to_odd[...] = choose(odd_chip, done2[0:72], done2[192:264])


def near_own_step(taps, n1, n2, n1_out, n2_out):
    for t in range(4):
        f = [n1[i, 8 * t : 8 * t + 8] for i in range(16)]
        for i in range(16):
            n1_out[i, 8 * t : 8 * t + 8] = sum(
                taps[0, a + 8] * f[i + a] for a in range(-8, 9) if 0 <= i + a < 16
            )
    for t in range(3):
        half = {j: n2[j + 1, 8 * t : 8 * t + 8] for j in range(-1, 10)}
        for i in range(-1, 10):
            n2_out[i + 1, 8 * t : 8 * t + 8] = sum(
                taps[1, a + 8] * half[i + a] for a in range(-8, 9) if i + a in half
            )


def near_x_step(taps, n1, n2, even2, odd2, high, low, y2, z2, out):
    odd_chip = lax.rem(lax.axis_index("gx") // 2, 2) == 1
    low2 = jnp.where(odd_chip, even2[...], odd2[...])
    high2 = jnp.where(odd_chip, odd2[...], even2[...])
    for t in range(4):
        f = {}
        for i in range(8):
            f[i - 8] = low[32 * i + 8 * t : 32 * i + 8 * t + 8]
            f[i + 16] = high[32 * i + 8 * t : 32 * i + 8 * t + 8]
        for i in range(16):
            total = n1[i, 8 * t : 8 * t + 8] + sum(taps[0, a + 8] * f[i + a] for a in range(-8, 9) if i + a in f)
            out[i, 8 * t : 8 * t + 8] = total
    tiles = {}
    for t in range(3):
        half = {}
        for j in range(-1, 10):
            at = 256 + 24 * (j + 1) + 8 * t
            for place, part in ((j - 8, low[at : at + 8]), (j + 8, high[at : at + 8])):
                half[place] = half[place] + part if place in half else part
        for k in range(3):
            at = 24 * k + 8 * t
            half[k - 9] = half[k - 9] + low2[at : at + 8]
            half[k + 15] = half[k + 15] + high2[at : at + 8]
        for i in range(-1, 10):
            total = n2[i + 1, 8 * t : 8 * t + 8] + sum(
                taps[1, a + 8] * half[i + a] for a in range(-8, 9) if i + a in half
            )
            tiles[i, t] = total
    tall = jnp.concatenate([tiles[i, t] for i in range(-1, 10) for t in range(3)], axis=0)
    tall = from_right(tall, z2)
    wide = from_left(y2, lanes([tall[24 * i : 24 * i + 24] for i in range(11)]))
    rows = raise_rows({i - 1: wide[:, 128 * i : 128 * i + 128] for i in range(11)}, 0, 15)
    for i in range(16):
        out[i] = out[i] + rows[i]


def top_step(gathered, wz1, wz2, my, out):
    whole = gathered[...].astype(f32).reshape(8, 8, 8, 128)
    rows = lanes([whole[:, g].reshape(64, 128) for g in range(8)]).astype(bf16)
    along_z = jnp.dot(rows, wz1[...], preferred_element_type=f32)
    along_z = along_z + jnp.dot(rows, wz2[...], preferred_element_type=f32)
    done = dot(my[...], along_z)
    row = iota((16, 128), 0)
    block, past = done[:, 0:128], jnp.where(iota((16, 128), 1) % 32 // 5 == row % 5, done[:, 128:256], 0.0)
    for t in range(3):
        mine = (row // 5 == t) & (row < 13)
        block = jnp.where(row == 13 + t, jnp.sum(jnp.where(mine, past, 0.0), axis=0, keepdims=True), block)
    out[...] = jnp.broadcast_to(block[None], (8, 16, 128))


def raise_rows(rows, first, last):
    out = {}
    for i in range(first, last + 1):
        if i % 2 == 0:
            out[i] = rows[i // 2]
        else:
            j = (i - 1) // 2
            out[i] = (9.0 / 16.0) * (rows[j] + rows[j + 1]) - (1.0 / 16.0) * (rows[j - 1] + rows[j + 2])
    return out


def last_step(top, wx, near, y_both, z_both, out):
    e3 = {}
    row, lane = iota((16, 128), 0), iota((16, 128), 1)
    here = (lane >= 32) & (lane < 57) & (lane % 32 // 5 == row % 5)
    for i in range(9):
        total = None
        for g in range(8):
            term = wx[i : i + 1, 128 * g : 128 * g + 128] * top[g]
            total = term if total is None else total + term
        total = total + pltpu.roll(total, 64, 1)
        total = total + pltpu.roll(total, 32, 1)
        past = jnp.where(row < 5, total[13:14], jnp.where(row < 10, total[14:15], total[15:16]))
        e3[i - 2] = jnp.where(lane < 32, total, jnp.where(here, past, 0.0))
    tall = from_right(jnp.concatenate([e3[i] for i in range(-2, 7)], axis=0), z_both)
    wide = from_left(y_both, lanes([tall[16 * i : 16 * i + 16] for i in range(9)]))
    rows = raise_rows({i - 2: wide[:, 128 * i : 128 * i + 128] for i in range(9)}, -1, 9)
    rows = raise_rows(rows, 0, 15)
    for i in range(16):
        out[i] = rows[i] + near[i]


def per_device(charge, kernel_taps, top_x, top_y, top_z):
    def shift(block, by):
        return lax.ppermute(block, "gx", [(i, (i + by) % 8) for i in range(8)])

    z_matrix = jnp.asarray(z_first, bf16)
    to_even, to_odd = call(y_send, [((224, 128), bf16)] * 2, [charge])
    from_odd = lax.ppermute(to_odd, "gy", swap_odd)
    from_even = lax.ppermute(to_even, "gy", swap_even)
    my1, my2 = call(
        prep_y, [((64, 48), bf16), ((32, 64), f32)], [kernel_taps, jnp.asarray(y_sources)], smem=(0,)
    )
    mz1, mz2 = call(prep_z, [((256, 128), f32)] * 2, [kernel_taps], smem=(0,))
    (own_share,) = call(own_step, [((11, 32, 128), f32)], [charge, z_matrix], after=[to_odd])
    wz1, wz2, ty, wx = call(
        prep_top,
        [((1024, 256), bf16)] * 2 + [((16, 64), f32), ((16, 1024), f32)],
        [top_x[None], top_y[None], top_z[None]],
    )

    n1, n2, q3, to_even, to_odd = call(
        y_step,
        [((16, 32, 128), f32), ((11, 24, 128), f32), ((9, 8, 128), f32), ((88, 128), f32), ((88, 128), f32)],
        [charge, from_odd, from_even, own_share, my1, my2, z_matrix, jnp.asarray(z_second, bf16)],
        after=[mz1, wx],
    )
    from_odd = lax.ppermute(to_odd, "gz", swap_odd)
    from_even = lax.ppermute(to_even, "gz", swap_even)

    q3, to_low, to_high = call(q3_z_step, [((8, 128), f32)] * 3, [q3, from_odd, from_even])
    (message,) = call(q3_x_step, [((32, 16, 128), bf16)], [shift(to_low, -1), q3, shift(to_high, 1)])
    gathered = lax.all_to_all(
        message.reshape(64, 8, 128), ("gy", "gz"), split_axis=0, concat_axis=0, tiled=True
    )
    n1, n2, to_low, to_high, to_even, to_odd = call(
        near_z_step,
        [((16, 32, 128), f32), ((11, 24, 128), f32)] + [((520, 128), f32)] * 2 + [((72, 128), f32)] * 2,
        [n1, n2, from_odd, from_even, mz1, mz2], after=[message],
    )
    halos = [
        lax.ppermute(to_even, "gx", [(0, 2), (2, 0), (1, 3), (3, 1), (4, 6), (6, 4), (5, 7), (7, 5)]),
        lax.ppermute(to_odd, "gx", [(2, 4), (4, 2), (3, 5), (5, 3), (6, 0), (0, 6), (7, 1), (1, 7)]),
        shift(to_low, -1),
        shift(to_high, 1),
    ]
    n1, n2 = call(
        near_own_step, [((16, 32, 128), f32), ((11, 24, 128), f32)], [kernel_taps, n1, n2], smem=(0,)
    )
    (near,) = call(
        near_x_step, [((16, 32, 128), f32)],
        [kernel_taps, n1, n2, *halos, jnp.asarray(y_raise, bf16), jnp.asarray(z_raise, bf16)], smem=(0,),
    )
    (message,) = call(top_step, [((8, 16, 128), f32)], [gathered, wz1, wz2, ty], after=[near])
    top = lax.all_to_all(message, "gx", split_axis=0, concat_axis=0, tiled=True)
    (result,) = call(
        last_step, [((16, 32, 128), f32)],
        [top, wx, near, jnp.asarray(y_raise_both, bf16), jnp.asarray(z_raise_both, bf16)],
    )
    return result


def solution(mesh):
    return jax.shard_map(
        per_device,
        mesh=mesh,
        in_specs=(P("gx", "gy", "gz"), P(), P(), P(), P()),
        out_specs=P("gx", "gy", "gz"),
        check_vma=False,
    )
```
